32 devices in a mesh: section: 4 (over z), expert: 8 (over y, x, core).
Axes of the slice: x: 2, y: 2, z: 4, core: 2. Of those that a mesh axis runs over, the one named last changes fastest.
Arguments:
- tokens: bfloat16 [8, 64, 2048], P(None, 'expert', 'section'), may hold values from -6 to 6
- norm_gain: float32 [4, 2048], P('section'), may hold values from 0.1 to 1.9
- gate_weight: bfloat16 [4, 32, 2048, 384], P('section', 'expert'), may hold values from -0.125 to 0.125
- up_weight: bfloat16 [4, 32, 2048, 384], P('section', 'expert'), may hold values from -0.125 to 0.125
- down_weight: bfloat16 [4, 32, 384, 2048], P('section', 'expert'), may hold values from -0.3125 to 0.3125
- expert_ids: int32 [4, 8, 64, 8], P('section', None, 'expert'), may hold values from 0 to 31, all different within a row; in each aligned block of 8 rows (0 to 7, 8 to 15, ..., all dimensions but the last counted through in order) at most 2 rows name the same one
- gate_probs: float32 [4, 8, 64, 8], P('section', None, 'expert'), may hold values from 0.05 to 1
Outputs:
- hidden_states: bfloat16 [4, 8, 64, 2048], P('section', None, 'expert')
The draws below stay inside these ranges and needn't reach their ends.
Inputs may be any that keep to these rules, and one draw needn't show every extreme that they name: `expert_ids`: in the 8 rows of one index of expert for one layer and micro-batch (aligned blocks of 8 rows), no expert is named by more than 2 rows, a bound that some block reaches in every draw.
All inputs are finite; a program needn't handle non-finite values.
Results may differ from the reference program's by a relative error of at most 0.04.
Values may be sent and summed in bfloat16 or wider, within the bound.
A program may use at most 64 MiB of HBM per device.

```python
import math
import jax
import jax.numpy as jnp
import numpy as np
from jax import lax

D = 2048
TOP = 8
FF = 384
EXPERTS = 32
MB = 8
ROWS_DEV = 8
CAP = 2
LAYERS = 4
TOKENS_MB = 64
N_EXPERT = 8


def levels(key, shape, split, low, high):
    loudness = 1.0
    for dim, parts in split:
        steps = jax.random.uniform(jax.random.fold_in(jax.random.fold_in(key, 6), dim), (parts,), jnp.float32, low / len(split), high / len(split))
        loudness = loudness * jnp.repeat(jnp.exp(steps), shape[dim] // parts).reshape((-1,) + (1,) * (len(shape) - 1 - dim))
    return loudness


def routed_block(rng, own, number, rows, count, top, bound, lean):
    ranking = jax.random.permutation(rng, count)
    crowded, ordinary = shares(count, rows * top, bound, lean, True), shares(count, rows * top, bound, lean, False)
    places = jnp.arange(count)

    def named(lengths, offset_by):
        used = int((lengths > 0).sum())
        fixed = max(1, used // 4)
        passed = fixed + (places - fixed + offset_by * (used - fixed)) % max(1, count - fixed)
        return jnp.zeros((count,), jnp.int32).at[ranking[jnp.where(places < fixed, places, passed)]].set(jnp.asarray(lengths, jnp.int32))

    lengths = jnp.where(number % 4 == 0, named(crowded, number // 4), named(ordinary, number - number // 4 - 1))
    mixed = jax.random.permutation(jax.random.fold_in(own, 3), count)
    giver, taker = mixed[0:count // 2 * 2:2], mixed[1:count // 2 * 2:2]
    margin = jnp.minimum(lengths[giver] - 1, bound - lengths[taker]) // 2
    margin = jnp.where((giver == ranking[0]) | (taker == ranking[0]) | (lengths[taker] == 0), 0, jnp.maximum(margin, 0))
    passed = jax.random.randint(jax.random.fold_in(own, 4), (count // 2,), 0, 1 << 20) % (margin + 1)
    lengths = lengths.at[giver].add(-passed).at[taker].add(passed)
    labels = jnp.searchsorted(jnp.cumsum(lengths), jnp.arange(rows * top), side="right").astype(jnp.int32)
    grid = labels.reshape(top, rows).T
    grid = grid[jax.random.permutation(jax.random.fold_in(own, 1), rows)]
    offset_by = jax.random.randint(jax.random.fold_in(own, 2), (rows, 1), 0, top)
    return jnp.take_along_axis(grid, (jnp.arange(top)[None, :] + offset_by) % top, axis=1)


def shares(amount, total, reach, slope, full):
    weights = [(1 << 20) // math.isqrt(standing ** slope) + 1 for standing in range(1, amount + 1)]
    largest = reach if full else min(reach, max(-(-total // amount), total * weights[0] // sum(weights)))
    least = 1 if total - largest >= amount - 1 else 0
    counts, spare = [largest] + [least] * (amount - 1), total - largest - least * (amount - 1)
    while spare > 0:
        movable = [i for i in range(1, amount) if counts[i] < largest] or [i for i in range(1, amount) if counts[i] < reach]
        mass, remaining = sum([weights[i] for i in movable]), spare
        for i in movable:
            addition = min(reach - counts[i], max(1, remaining * weights[i] // mass), spare)
            counts[i] = counts[i] + addition
            spare = spare - addition
    return np.array(counts)


def centred(rng, extent, spread, bound, shards=(), kind=jnp.bfloat16):
    result = spread * jax.random.normal(rng, extent, jnp.float32)
    if shards:
        result = result * levels(rng, extent, shards, -0.22, 0.18)
    return jnp.clip(result, -bound, bound).astype(kind)


def setup_inputs(seed: int = 0) -> dict:
    splits = jax.random.split(jax.random.key(seed), 8)
    tokens = centred(splits[0], (MB, TOKENS_MB, D), 1.0, 6.0, ((1, 8), (2, 4)))
    norm_gain = jnp.clip(1.0 + 0.18 * jax.random.normal(splits[1], (LAYERS, D), jnp.float32), 0.1, 1.9)
    gate_weight = centred(splits[2], (LAYERS, EXPERTS, D, FF), D ** -0.5, 0.125, ((0, 4), (1, 8)))
    up_weight = centred(splits[3], (LAYERS, EXPERTS, D, FF), D ** -0.5, 0.125, ((0, 4), (1, 8)))
    down_weight = centred(splits[4], (LAYERS, EXPERTS, FF, D), FF ** -0.5, 0.3125, ((0, 4), (1, 8)))
    expert_ids_keys = jax.random.split(jax.random.fold_in(splits[5], 1), LAYERS * MB * TOKENS_MB // ROWS_DEV)
    expert_ids_turns = jax.random.permutation(jax.random.fold_in(splits[5], 3), LAYERS * MB * TOKENS_MB // ROWS_DEV)
    expert_ids = jax.vmap(lambda own, number: routed_block(jax.random.fold_in(splits[5], 2), own, number, ROWS_DEV, EXPERTS, TOP, CAP, 2))(expert_ids_keys, expert_ids_turns).reshape((LAYERS, MB, TOKENS_MB, TOP))
    gate_probs = jnp.clip(jnp.exp(math.log(1.0) - 2.9957323 * jax.random.uniform(splits[6], (LAYERS, MB, TOKENS_MB, TOP), jnp.float32) ** levels(splits[6], (LAYERS, MB, TOKENS_MB, TOP), ((0, 4), (2, 8)), -0.2, 0.2)), 0.05, 1.0)
    return {"tokens": tokens, "norm_gain": norm_gain, "gate_weight": gate_weight, "up_weight": up_weight, "down_weight": down_weight, "expert_ids": expert_ids, "gate_probs": gate_probs}


EPS = 1e-06

def expert_rows(args):
    routed, w_gate, w_up, w_down = args
    gate_proj = jnp.dot(routed, w_gate, preferred_element_type=jnp.float32)
    up_proj = jnp.dot(routed, w_up, preferred_element_type=jnp.float32)
    active = (jax.nn.silu(gate_proj) * up_proj).astype(jnp.bfloat16)
    return jnp.dot(active, w_down, preferred_element_type=jnp.float32).astype(jnp.bfloat16)

def slot_numbers(flat_ids):
    onehot = (flat_ids[:, :, None] == jnp.arange(EXPERTS, dtype=jnp.int32)[None, None, :]).astype(jnp.int32)
    before = jnp.cumsum(onehot, axis=1) - onehot
    return flat_ids * CAP + lax.optimization_barrier(jnp.sum(onehot * before, axis=2))

def moe_layer(layer_input, norm_scale, expert_list, gate_share, w_gate, w_up, w_down):
    total_rows = layer_input.shape[0]
    blocks = N_EXPERT
    row_count = total_rows // blocks
    top_count = expert_list.shape[1]
    widened = layer_input.astype(jnp.float32)
    normed = (widened * lax.rsqrt(lax.optimization_barrier(jnp.mean(widened * widened, axis=-1, keepdims=True)) + EPS) * norm_scale).astype(jnp.bfloat16)
    weight = gate_share / lax.optimization_barrier(jnp.sum(gate_share, axis=-1, keepdims=True))
    slot_index = slot_numbers(expert_list.reshape(blocks, row_count * top_count)).reshape(blocks, row_count, top_count)
    target = jnp.arange(EXPERTS * CAP, dtype=jnp.int32)
    placement = lax.optimization_barrier(jnp.sum((slot_index[:, None, :, :] == target[None, :, None, None]).astype(jnp.float32), axis=3))
    normed_blocks = normed.astype(jnp.float32).reshape(blocks, row_count, D)
    buffer = jnp.einsum('bjr,brd->bjd', placement, normed_blocks, precision=lax.Precision.HIGHEST)
    buffer = buffer.reshape(blocks, EXPERTS, CAP, D).transpose(1, 0, 2, 3).reshape(EXPERTS, blocks * CAP, D).astype(jnp.bfloat16)
    outputs = lax.map(expert_rows, (buffer, w_gate, w_up, w_down))
    flat_out = outputs.reshape(EXPERTS * blocks * CAP, D)
    block_of = (jnp.arange(total_rows, dtype=jnp.int32) // row_count)[:, None]
    position = slot_index.reshape(total_rows, top_count) - expert_list * CAP
    index = (expert_list * (blocks * CAP) + block_of * CAP + position).astype(jnp.int32)
    picked = jnp.take(flat_out, index.reshape(-1), axis=0).astype(jnp.float32).reshape(total_rows, top_count, D)
    mixed = lax.optimization_barrier(jnp.sum(weight[:, :, None] * picked, axis=1))
    return (widened + mixed).astype(jnp.bfloat16)

def reference(tokens, norm_gain, gate_weight, up_weight, down_weight, expert_ids, gate_probs):
    current = tokens
    collected = []
    for layer_index in range(LAYERS):
        outputs = []
        for micro_index in range(MB):
            outputs.append(moe_layer(current[micro_index], norm_gain[layer_index], expert_ids[layer_index, micro_index], gate_probs[layer_index, micro_index], gate_weight[layer_index], up_weight[layer_index], down_weight[layer_index]))
        current = jnp.stack(outputs)
        collected.append(current)
    return jnp.stack(collected)
```

```python
import functools

import jax
import jax.numpy as jnp
from jax import lax
from jax.experimental import pallas as pl
from jax.experimental.pallas import tpu as pltpu
from jax.sharding import PartitionSpec as P

EPS = 1e-06
GROUP = 2
MESH = pl.DeviceIdType.MESH
LANES = 128


def kernel(
    sections, peers, experts_local,
    tokens, gain, gate_hbm, up_hbm, down_hbm, ids, probs,
    out,
    w_gate, w_up, w_down, x_in, normed, active, partial, pair_in, pair_out, returned, shares,
    weight_sem, token_send, token_recv, share_send, share_recv, gather_send, gather_recv,
    forward_send, pair_send, pair_recv, return_send, return_recv, pass_send, pass_recv,
):
    groups, rows, width = x_in.shape
    chips = peers // 2
    ff = gate_hbm.shape[2]
    hidden = experts_local * ff
    experts = experts_local * peers
    part = tokens.shape[2]
    section = lax.axis_index("section")
    index = lax.axis_index("expert")
    chip, core = lax.div(index, 2), lax.rem(index, 2)
    other = 1 - core
    sibling = chip * 2 + other

    def slot_of(chip_index, core_index):
        return core_index * chips + chip_index

    mine = slot_of(chip, core)

    def weight_copies(which):
        copies = []
        for e in range(experts_local):
            span = pl.ds(e * ff, ff)
            if which < 2:
                source, target = ((gate_hbm, w_gate), (up_hbm, w_up))[which]
                copies.append(pltpu.make_async_copy(
                    source.at[e], target.at[:, span], weight_sem.at[which, e]))
            else:
                copies.append(pltpu.make_async_copy(
                    down_hbm.at[e], w_down.at[span], weight_sem.at[which, e]))
        return copies

    for copy in weight_copies(0) + weight_copies(1) + weight_copies(2):
        copy.start()

    def remote(source, target, send, recv, device):
        return pltpu.make_async_remote_copy(
            src_ref=source, dst_ref=target, send_sem=send, recv_sem=recv,
            device_id=device, device_id_type=MESH)

    def at_peer(peer):
        return {"section": section, "expert": peer}

    def at_section(which):
        return {"section": which, "expert": index}

    barrier = pltpu.get_barrier_semaphore()
    for step in range(1, peers):
        pl.semaphore_signal(barrier, inc=1, device_id=at_peer(lax.rem(index + step, peers)),
                            device_id_type=MESH)
    for step in range(1, sections):
        pl.semaphore_signal(barrier, inc=1,
                            device_id=at_section(lax.rem(section + step, sections)),
                            device_id_type=MESH)
    pl.semaphore_wait(barrier, peers + sections - 2)

    def token_copy(g, origin):
        columns = pl.ds(pl.multiple_of(origin * part, part), part)
        return remote(tokens.at[g], x_in.at[g, :, columns], token_send.at[g],
                      token_recv.at[g, origin], at_section(0))

    @pl.when(section > 0)
    def _():
        for g in range(groups):
            token_copy(g, section).start()

    lane = lax.broadcasted_iota(jnp.int32, (rows, LANES), 1)
    spread = jnp.zeros((rows, LANES), jnp.float32)
    top = ids.shape[2]
    for g in range(groups):
        share = probs[g] / jnp.sum(probs[g], axis=-1, keepdims=True)
        named = ids[g] + g * experts
        for k in range(top):
            spread += jnp.where(named[:, k:k + 1] == lane, share[:, k:k + 1], 0.0)
    shares[mine] = spread

    def share_copy(step):
        target = lax.rem(index + step, peers)
        return remote(shares.at[mine], shares.at[mine], share_send.at[step],
                      share_recv.at[mine], at_peer(target))

    def gather_copy(g, step):
        target = lax.rem(chip + step, chips) * 2 + core
        return remote(normed.at[g, mine], normed.at[g, mine], gather_send.at[g, step],
                      gather_recv.at[g, mine], at_peer(target))

    def sibling_copy(g):
        return remote(normed.at[g, mine], normed.at[g, mine], gather_send.at[g, 0],
                      gather_recv.at[g, mine], at_peer(sibling))

    def forward_copy(g, step):
        slot = slot_of(lax.rem(chip + step, chips), core)
        return remote(normed.at[g, slot], normed.at[g, slot], forward_send.at[g, step],
                      gather_recv.at[g, slot], at_peer(sibling))

    def gather_arrival(g, slot):
        return remote(normed.at[g, slot], normed.at[g, slot], gather_send.at[g, 0],
                      gather_recv.at[g, slot], at_peer(sibling))

    def pair_copy(g):
        return remote(partial.at[g, pl.ds(other * chips, chips)], pair_in.at[g],
                      pair_send.at[g], pair_recv.at[g], at_peer(sibling))

    def return_copy(g, step):
        target = lax.rem(chip + step, chips)
        return remote(pair_out.at[g, target], returned.at[g, chip], return_send.at[g, step],
                      return_recv.at[g, chip], at_peer(target * 2 + core))

    def return_arrival(g, origin):
        return remote(pair_out.at[g, origin], returned.at[g, origin], return_send.at[g, 0],
                      return_recv.at[g, origin], at_peer(sibling))

    def pass_copy(g):
        return remote(out.at[g], x_in.at[g], pass_send.at[g], pass_recv.at[g],
                      at_section(lax.rem(section + 1, sections)))

    def enter(g):
        @pl.when(section == 0)
        def _():
            x_in[g, :, pl.ds(0, part)] = tokens[g]
            for origin in range(1, sections):
                token_copy(g, origin).wait_recv()

        @pl.when(section > 0)
        def _():
            pass_copy(g).wait_recv()

        wide = x_in[g].astype(jnp.float32)
        scale = lax.rsqrt(jnp.mean(wide * wide, axis=-1, keepdims=True) + EPS)
        normed[g, mine] = (wide * scale * gain[...]).astype(jnp.bfloat16)
        for step in range(1, chips):
            gather_copy(g, step).start()
        sibling_copy(g).start()

    def forward(g):
        for step in range(1, chips):
            gather_arrival(g, slot_of(lax.rem(chip + step, chips), core)).wait_recv()
            forward_copy(g, step).start()

    total_rows = peers * rows
    tile = 256 if hidden % 256 == 0 else LANES
    wide_lane = lax.broadcasted_iota(jnp.int32, (total_rows, LANES), 1)

    def experts_block(g):
        for step in range(chips):
            gather_arrival(g, slot_of(lax.rem(chip + step, chips), other)).wait_recv()

        @pl.when(g == 0)
        def _():
            for copy in weight_copies(0) + weight_copies(1):
                copy.wait()
            for step in range(1, peers):
                origin = lax.rem(index + step, peers)
                slot = slot_of(lax.div(origin, 2), lax.rem(origin, 2))
                remote(shares.at[slot], shares.at[slot], share_send.at[step],
                       share_recv.at[slot], at_peer(origin)).wait_recv()

        every = shares[...].reshape(total_rows, LANES)
        factor = []
        for e in range(experts_local):
            pick = wide_lane == g * experts + index * experts_local + e
            factor.append(jnp.sum(jnp.where(pick, every, 0.0), axis=-1, keepdims=True))
        rows_in = normed[g].reshape(total_rows, width)
        for start in range(0, hidden, tile):
            columns = pl.ds(start, tile)
            gate = jnp.dot(rows_in, w_gate[:, columns], preferred_element_type=jnp.float32)
            up = jnp.dot(rows_in, w_up[:, columns], preferred_element_type=jnp.float32)
            mid = gate / (1.0 + jnp.exp(-gate)) * up
            for begin in range(0, tile, LANES):
                piece = mid[:, begin:begin + LANES] * factor[(start + begin) // ff]
                active[:, pl.ds(start + begin, LANES)] = piece.astype(jnp.bfloat16)

        @pl.when(g == 0)
        def _():
            for copy in weight_copies(2):
                copy.wait()

        acts = active[...]
        for start in range(0, width, 256):
            columns = pl.ds(start, 256)
            result = jnp.dot(acts, w_down[:, columns], preferred_element_type=jnp.float32)
            partial[g, :, :, columns] = result.astype(jnp.bfloat16).reshape(peers, rows, 256)
        pair_copy(g).start()

    def combine(g):
        pair_copy(g).wait_recv()
        for step in range(1, chips + 1):
            target = lax.rem(chip + step, chips)
            both = (partial[g, slot_of(target, core)].astype(jnp.float32)
                    + pair_in[g, target].astype(jnp.float32)).astype(jnp.bfloat16)
            pair_out[g, target] = both
            if step < chips:
                return_copy(g, step).start()

    def leave(g):
        total = x_in[g].astype(jnp.float32) + pair_out[g, chip].astype(jnp.float32)
        for step in range(1, chips):
            origin = lax.rem(chip + step, chips)
            return_arrival(g, origin).wait_recv()
            total += returned[g, origin].astype(jnp.float32)
        out[g] = total.astype(jnp.bfloat16)

        @pl.when(section < sections - 1)
        def _():
            pass_copy(g).start()

    for step in range(1, peers):
        share_copy(step).start()

    def one(g, carry):
        enter(g)
        forward(g)
        experts_block(g)
        combine(g)
        leave(g)
        return carry

    lax.fori_loop(0, groups, one, 0)

    for step in range(1, peers):
        share_copy(step).wait_send()

    def drain(g, carry):
        @pl.when(section > 0)
        def _():
            token_copy(g, section).wait_send()

        @pl.when(section < sections - 1)
        def _():
            pass_copy(g).wait_send()

        sibling_copy(g).wait_send()
        pair_copy(g).wait_send()
        for step in range(1, chips):
            gather_copy(g, step).wait_send()
            forward_copy(g, step).wait_send()
            return_copy(g, step).wait_send()
        return carry

    lax.fori_loop(0, groups, drain, 0)


def local(sections, peers, tokens, norm_gain, gate_weight, up_weight, down_weight, expert_ids,
          gate_probs):
    micro, rows_each, part = tokens.shape
    width = norm_gain.shape[1]
    groups, rows = micro // GROUP, rows_each * GROUP
    experts_local, ff = gate_weight.shape[1], gate_weight.shape[3]
    hidden = experts_local * ff
    top = expert_ids.shape[3]
    chips = peers // 2
    vmem = pl.BlockSpec(memory_space=pltpu.VMEM)
    anywhere = pl.BlockSpec(memory_space=pl.ANY)
    dma = pltpu.SemaphoreType.DMA
    bf16 = jnp.bfloat16
    result = pl.pallas_call(
        functools.partial(kernel, sections, peers, experts_local),
        out_shape=jax.ShapeDtypeStruct((groups, rows, width), bf16),
        in_specs=[vmem, vmem, anywhere, anywhere, anywhere, vmem, vmem],
        out_specs=vmem,
        scratch_shapes=[
            pltpu.VMEM((width, hidden), bf16),
            pltpu.VMEM((width, hidden), bf16),
            pltpu.VMEM((hidden, width), bf16),
            pltpu.VMEM((groups, rows, width), bf16),
            pltpu.VMEM((groups, peers, rows, width), bf16),
            pltpu.VMEM((peers * rows, hidden), bf16),
            pltpu.VMEM((groups, peers, rows, width), bf16),
            pltpu.VMEM((groups, chips, rows, width), bf16),
            pltpu.VMEM((groups, chips, rows, width), bf16),
            pltpu.VMEM((groups, chips, rows, width), bf16),
            pltpu.VMEM((peers, rows, LANES), jnp.float32),
            dma((3, experts_local)),
            dma((groups,)),
            dma((groups, sections)),
            dma((peers,)),
            dma((peers,)),
            dma((groups, chips)),
            dma((groups, peers)),
            dma((groups, chips)),
            dma((groups,)),
            dma((groups,)),
            dma((groups, chips)),
            dma((groups, chips)),
            dma((groups,)),
            dma((groups,)),
        ],
        compiler_params=pltpu.CompilerParams(
            collective_id=0, has_side_effects=True, vmem_limit_bytes=58 * 2**20
        ),
    )(
        tokens.reshape(groups, rows, part),
        norm_gain,
        gate_weight[0],
        up_weight[0],
        down_weight[0],
        expert_ids[0].reshape(groups, rows, top),
        gate_probs[0].reshape(groups, rows, top),
    )
    return result.reshape(1, micro, rows_each, width)


def solution(mesh):
    in_specs = (
        P(None, "expert", "section"),
        P("section", None),
        P("section", "expert", None, None),
        P("section", "expert", None, None),
        P("section", "expert", None, None),
        P("section", None, "expert", None),
        P("section", None, "expert", None),
    )
    out_specs = P("section", None, "expert", None)
    body = functools.partial(local, mesh.shape["section"], mesh.shape["expert"])
    return jax.shard_map(body, mesh=mesh, in_specs=in_specs, out_specs=out_specs, check_vma=False)
```

```python
import functools

import jax
import jax.numpy as jnp
from jax import lax
from jax.experimental import pallas as pl
from jax.experimental.pallas import tpu as pltpu
from jax.sharding import PartitionSpec as P

EPS = 1e-06
GROUP = 2
HALVES = 2
MESH = pl.DeviceIdType.MESH
LANES = 128


def kernel(
    sections, peers, experts_local,
    tokens, gain, gate_hbm, up_hbm, down_hbm, ids, probs,
    out,
    w_gate, w_up, w_down, x_in, normed, active, partial, pair_in, pair_out, returned, shares,
    weight_sem, token_send, token_recv, share_send, share_recv, gather_send, gather_recv,
    forward_send, pair_send, pair_recv, return_send, return_recv, pass_send, pass_recv,
):
    groups, rows, width = x_in.shape
    chips = peers // 2
    ff = gate_hbm.shape[2]
    hidden = experts_local * ff
    experts = experts_local * peers
    part = tokens.shape[2]
    section = lax.axis_index("section")
    index = lax.axis_index("expert")
    chip, core = lax.div(index, 2), lax.rem(index, 2)
    other = 1 - core
    sibling = chip * 2 + other

    def slot_of(chip_index, core_index):
        return core_index * chips + chip_index

    mine = slot_of(chip, core)

    def weight_copies(which):
        copies = []
        for e in range(experts_local):
            span = pl.ds(e * ff, ff)
            if which < 2:
                source, target = ((gate_hbm, w_gate), (up_hbm, w_up))[which]
                copies.append(pltpu.make_async_copy(
                    source.at[e], target.at[:, span], weight_sem.at[which, e]))
            else:
                copies.append(pltpu.make_async_copy(
                    down_hbm.at[e], w_down.at[span], weight_sem.at[which, e]))
        return copies

    for copy in weight_copies(0) + weight_copies(1) + weight_copies(2):
        copy.start()

    def remote(source, target, send, recv, device):
        return pltpu.make_async_remote_copy(
            src_ref=source, dst_ref=target, send_sem=send, recv_sem=recv,
            device_id=device, device_id_type=MESH)

    def at_peer(peer):
        return {"section": section, "expert": peer}

    def at_section(which):
        return {"section": which, "expert": index}

    barrier = pltpu.get_barrier_semaphore()
    for step in range(1, peers):
        pl.semaphore_signal(barrier, inc=1, device_id=at_peer(lax.rem(index + step, peers)),
                            device_id_type=MESH)
    for step in range(1, sections):
        pl.semaphore_signal(barrier, inc=1,
                            device_id=at_section(lax.rem(section + step, sections)),
                            device_id_type=MESH)
    pl.semaphore_wait(barrier, peers + sections - 2)

    def token_copy(g, origin):
        columns = pl.ds(pl.multiple_of(origin * part, part), part)
        return remote(tokens.at[g], x_in.at[g, :, columns], token_send.at[g],
                      token_recv.at[g, origin], at_section(0))

    @pl.when(section > 0)
    def _():
        for g in range(groups):
            token_copy(g, section).start()

    lane = lax.broadcasted_iota(jnp.int32, (rows, LANES), 1)
    spread = jnp.zeros((rows, LANES), jnp.float32)
    top = ids.shape[2]
    for g in range(groups):
        share = probs[g] / jnp.sum(probs[g], axis=-1, keepdims=True)
        named = ids[g] + g * experts
        for k in range(top):
            spread += jnp.where(named[:, k:k + 1] == lane, share[:, k:k + 1], 0.0)
    shares[mine] = spread

    def share_copy(step):
        target = lax.rem(index + step, peers)
        return remote(shares.at[mine], shares.at[mine], share_send.at[step],
                      share_recv.at[mine], at_peer(target))

    def gather_copy(g, step):
        target = lax.rem(chip + step, chips) * 2 + core
        return remote(normed.at[g, mine], normed.at[g, mine], gather_send.at[g, step],
                      gather_recv.at[g, mine], at_peer(target))

    def sibling_copy(g):
        return remote(normed.at[g, mine], normed.at[g, mine], gather_send.at[g, 0],
                      gather_recv.at[g, mine], at_peer(sibling))

    def forward_copy(g, step):
        slot = slot_of(lax.rem(chip + step, chips), core)
        return remote(normed.at[g, slot], normed.at[g, slot], forward_send.at[g, step],
                      gather_recv.at[g, slot], at_peer(sibling))

    def gather_arrival(g, slot):
        return remote(normed.at[g, slot], normed.at[g, slot], gather_send.at[g, 0],
                      gather_recv.at[g, slot], at_peer(sibling))

    half = width // HALVES

    def pair_copy(g, h):
        return remote(partial.at[g, h, pl.ds(other * chips, chips)], pair_in.at[g, h],
                      pair_send.at[g, h], pair_recv.at[g, h], at_peer(sibling))

    def return_copy(g, h, step):
        target = lax.rem(chip + step, chips)
        return remote(pair_out.at[g, h, target], returned.at[g, h, chip],
                      return_send.at[g, h, step], return_recv.at[g, h, chip],
                      at_peer(target * 2 + core))

    def return_arrival(g, h, origin):
        return remote(pair_out.at[g, h, origin], returned.at[g, h, origin],
                      return_send.at[g, h, 0], return_recv.at[g, h, origin], at_peer(sibling))

    def pass_copy(g, h):
        columns = pl.ds(h * half, half)
        return remote(out.at[g, :, columns], x_in.at[g, :, columns], pass_send.at[g, h],
                      pass_recv.at[g, h], at_section(lax.rem(section + 1, sections)))

    def enter(g):
        @pl.when(section == 0)
        def _():
            x_in[g, :, pl.ds(0, part)] = tokens[g]
            for origin in range(1, sections):
                token_copy(g, origin).wait_recv()

        @pl.when(section > 0)
        def _():
            for h in range(HALVES):
                pass_copy(g, h).wait_recv()

        wide = x_in[g].astype(jnp.float32)
        scale = lax.rsqrt(jnp.mean(wide * wide, axis=-1, keepdims=True) + EPS)
        normed[g, mine] = (wide * scale * gain[...]).astype(jnp.bfloat16)
        for step in range(1, chips):
            gather_copy(g, step).start()
        sibling_copy(g).start()

    def forward(g):
        for step in range(1, chips):
            gather_arrival(g, slot_of(lax.rem(chip + step, chips), core)).wait_recv()
            forward_copy(g, step).start()

    total_rows = peers * rows
    tile = 256 if hidden % 256 == 0 else LANES
    wide_lane = lax.broadcasted_iota(jnp.int32, (total_rows, LANES), 1)

    def project_in(g):
        for step in range(chips):
            gather_arrival(g, slot_of(lax.rem(chip + step, chips), other)).wait_recv()

        @pl.when(g == 0)
        def _():
            for copy in weight_copies(0) + weight_copies(1):
                copy.wait()
            for step in range(1, peers):
                origin = lax.rem(index + step, peers)
                slot = slot_of(lax.div(origin, 2), lax.rem(origin, 2))
                remote(shares.at[slot], shares.at[slot], share_send.at[step],
                       share_recv.at[slot], at_peer(origin)).wait_recv()

        every = shares[...].reshape(total_rows, LANES)
        factor = []
        for e in range(experts_local):
            pick = wide_lane == g * experts + index * experts_local + e
            factor.append(jnp.sum(jnp.where(pick, every, 0.0), axis=-1, keepdims=True))
        rows_in = normed[g].reshape(total_rows, width)
        for start in range(0, hidden, tile):
            if start == hidden // tile // 2 * tile:
                @pl.when(g > 0)
                def _():
                    for h in range(HALVES):
                        leave(g - 1, h)

            columns = pl.ds(start, tile)
            gate = jnp.dot(rows_in, w_gate[:, columns], preferred_element_type=jnp.float32)
            up = jnp.dot(rows_in, w_up[:, columns], preferred_element_type=jnp.float32)
            mid = gate / (1.0 + jnp.exp(-gate)) * up
            for begin in range(0, tile, LANES):
                piece = mid[:, begin:begin + LANES] * factor[(start + begin) // ff]
                active[:, pl.ds(start + begin, LANES)] = piece.astype(jnp.bfloat16)

    def project_out(g, h):
        if h == 0:
            @pl.when(g == 0)
            def _():
                for copy in weight_copies(2):
                    copy.wait()

        acts = active[...]
        for start in range(0, half, 256):
            columns = pl.ds(h * half + start, 256)
            result = jnp.dot(acts, w_down[:, columns], preferred_element_type=jnp.float32)
            partial[g, h, :, :, pl.ds(start, 256)] = (
                result.astype(jnp.bfloat16).reshape(peers, rows, 256))
        pair_copy(g, h).start()

    def combine(g, h):
        pair_copy(g, h).wait_recv()
        for step in range(1, chips + 1):
            target = lax.rem(chip + step, chips)
            both = (partial[g, h, slot_of(target, core)].astype(jnp.float32)
                    + pair_in[g, h, target].astype(jnp.float32)).astype(jnp.bfloat16)
            pair_out[g, h, target] = both
            if step < chips:
                return_copy(g, h, step).start()

    def leave(g, h):
        columns = pl.ds(h * half, half)
        total = x_in[g, :, columns].astype(jnp.float32) + pair_out[g, h, chip].astype(jnp.float32)
        for step in range(1, chips):
            origin = lax.rem(chip + step, chips)
            return_arrival(g, h, origin).wait_recv()
            total += returned[g, h, origin].astype(jnp.float32)
        out[g, :, columns] = total.astype(jnp.bfloat16)

        @pl.when(section < sections - 1)
        def _():
            pass_copy(g, h).start()

    for step in range(1, peers):
        share_copy(step).start()

    enter(0)
    forward(0)

    def one(g, carry):
        project_in(g)

        @pl.when(g < groups - 1)
        def _():
            enter(g + 1)

        for h in range(HALVES):
            project_out(g, h)
        for h in range(HALVES):
            combine(g, h)

        @pl.when(g < groups - 1)
        def _():
            forward(g + 1)

        return carry

    lax.fori_loop(0, groups, one, 0)
    for h in range(HALVES):
        leave(groups - 1, h)

    for step in range(1, peers):
        share_copy(step).wait_send()

    def drain(g, carry):
        @pl.when(section > 0)
        def _():
            token_copy(g, section).wait_send()

        @pl.when(section < sections - 1)
        def _():
            for h in range(HALVES):
                pass_copy(g, h).wait_send()

        sibling_copy(g).wait_send()
        for step in range(1, chips):
            gather_copy(g, step).wait_send()
            forward_copy(g, step).wait_send()
        for h in range(HALVES):
            pair_copy(g, h).wait_send()
            for step in range(1, chips):
                return_copy(g, h, step).wait_send()
        return carry

    lax.fori_loop(0, groups, drain, 0)


def local(sections, peers, tokens, norm_gain, gate_weight, up_weight, down_weight, expert_ids,
          gate_probs):
    micro, rows_each, part = tokens.shape
    width = norm_gain.shape[1]
    groups, rows = micro // GROUP, rows_each * GROUP
    experts_local, ff = gate_weight.shape[1], gate_weight.shape[3]
    hidden = experts_local * ff
    top = expert_ids.shape[3]
    chips = peers // 2
    vmem = pl.BlockSpec(memory_space=pltpu.VMEM)
    anywhere = pl.BlockSpec(memory_space=pl.ANY)
    dma = pltpu.SemaphoreType.DMA
    bf16 = jnp.bfloat16
    result = pl.pallas_call(
        functools.partial(kernel, sections, peers, experts_local),
        out_shape=jax.ShapeDtypeStruct((groups, rows, width), bf16),
        in_specs=[vmem, vmem, anywhere, anywhere, anywhere, vmem, vmem],
        out_specs=vmem,
        scratch_shapes=[
            pltpu.VMEM((width, hidden), bf16),
            pltpu.VMEM((width, hidden), bf16),
            pltpu.VMEM((hidden, width), bf16),
            pltpu.VMEM((groups, rows, width), bf16),
            pltpu.VMEM((groups, peers, rows, width), bf16),
            pltpu.VMEM((peers * rows, hidden), bf16),
            pltpu.VMEM((groups, HALVES, peers, rows, width // HALVES), bf16),
            pltpu.VMEM((groups, HALVES, chips, rows, width // HALVES), bf16),
            pltpu.VMEM((groups, HALVES, chips, rows, width // HALVES), bf16),
            pltpu.VMEM((groups, HALVES, chips, rows, width // HALVES), bf16),
            pltpu.VMEM((peers, rows, LANES), jnp.float32),
            dma((3, experts_local)),
            dma((groups,)),
            dma((groups, sections)),
            dma((peers,)),
            dma((peers,)),
            dma((groups, chips)),
            dma((groups, peers)),
            dma((groups, chips)),
            dma((groups, HALVES)),
            dma((groups, HALVES)),
            dma((groups, HALVES, chips)),
            dma((groups, HALVES, chips)),
            dma((groups, HALVES)),
            dma((groups, HALVES)),
        ],
        compiler_params=pltpu.CompilerParams(
            collective_id=0, has_side_effects=True, vmem_limit_bytes=58 * 2**20
        ),
    )(
        tokens.reshape(groups, rows, part),
        norm_gain,
        gate_weight[0],
        up_weight[0],
        down_weight[0],
        expert_ids[0].reshape(groups, rows, top),
        gate_probs[0].reshape(groups, rows, top),
    )
    return result.reshape(1, micro, rows_each, width)


def solution(mesh):
    in_specs = (
        P(None, "expert", "section"),
        P("section", None),
        P("section", "expert", None, None),
        P("section", "expert", None, None),
        P("section", "expert", None, None),
        P("section", None, "expert", None),
        P("section", None, "expert", None),
    )
    out_specs = P("section", None, "expert", None)
    body = functools.partial(local, mesh.shape["section"], mesh.shape["expert"])
    return jax.shard_map(body, mesh=mesh, in_specs=in_specs, out_specs=out_specs, check_vma=False)
```

```python
import functools

import jax
import jax.numpy as jnp
from jax import lax
from jax.experimental import pallas as pl
from jax.experimental.pallas import tpu as pltpu
from jax.sharding import PartitionSpec as P

EPS = 1e-06
GROUP = 2
HALVES = 2
MESH = pl.DeviceIdType.MESH
LANES = 128


def kernel(
    sections, peers, experts_local,
    tokens, gain, gate_hbm, up_hbm, down_hbm, ids, probs,
    out,
    w_gate, w_up, w_down, x_in, normed, active, partial, pair_in, pair_out, returned, shares,
    weight_sem, token_send, token_recv, share_send, share_recv, gather_send, gather_recv,
    forward_send, pair_send, pair_recv, return_send, return_recv, pass_send, pass_recv,
):
    groups, rows, width = x_in.shape
    chips = peers // 2
    ff = gate_hbm.shape[2]
    hidden = experts_local * ff
    experts = experts_local * peers
    part = tokens.shape[2]
    section = lax.axis_index("section")
    index = lax.axis_index("expert")
    chip, core = lax.div(index, 2), lax.rem(index, 2)
    other = 1 - core
    sibling = chip * 2 + other

    def slot_of(chip_index, core_index):
        return core_index * chips + chip_index

    mine = slot_of(chip, core)

    def weight_copies(which):
        copies = []
        for e in range(experts_local):
            span = pl.ds(e * ff, ff)
            if which < 2:
                source, target = ((gate_hbm, w_gate), (up_hbm, w_up))[which]
                copies.append(pltpu.make_async_copy(
                    source.at[e], target.at[:, span], weight_sem.at[which, e]))
            else:
                copies.append(pltpu.make_async_copy(
                    down_hbm.at[e], w_down.at[span], weight_sem.at[which, e]))
        return copies

    for copy in weight_copies(0) + weight_copies(1) + weight_copies(2):
        copy.start()

    def remote(source, target, send, recv, device):
        return pltpu.make_async_remote_copy(
            src_ref=source, dst_ref=target, send_sem=send, recv_sem=recv,
            device_id=device, device_id_type=MESH)

    def at_peer(peer):
        return {"section": section, "expert": peer}

    def at_section(which):
        return {"section": which, "expert": index}

    barrier = pltpu.get_barrier_semaphore()
    for step in range(1, peers):
        pl.semaphore_signal(barrier, inc=1, device_id=at_peer(lax.rem(index + step, peers)),
                            device_id_type=MESH)
    for step in range(1, sections):
        pl.semaphore_signal(barrier, inc=1,
                            device_id=at_section(lax.rem(section + step, sections)),
                            device_id_type=MESH)
    pl.semaphore_wait(barrier, peers + sections - 2)

    def token_copy(g, origin):
        columns = pl.ds(pl.multiple_of(origin * part, part), part)
        return remote(tokens.at[g], x_in.at[g, :, columns], token_send.at[g],
                      token_recv.at[g, origin], at_section(0))

    @pl.when(section > 0)
    def _():
        for g in range(groups):
            token_copy(g, section).start()

    lane = lax.broadcasted_iota(jnp.int32, (rows, LANES), 1)
    spread = jnp.zeros((rows, LANES), jnp.float32)
    top = ids.shape[2]
    for g in range(groups):
        share = probs[g] / jnp.sum(probs[g], axis=-1, keepdims=True)
        named = ids[g] + g * experts
        for k in range(top):
            spread += jnp.where(named[:, k:k + 1] == lane, share[:, k:k + 1], 0.0)
    shares[mine] = spread

    def share_copy(step):
        target = lax.rem(index + step, peers)
        return remote(shares.at[mine], shares.at[mine], share_send.at[step],
                      share_recv.at[mine], at_peer(target))

    def gather_copy(g, step):
        target = lax.rem(chip + step, chips) * 2 + core
        return remote(normed.at[g, mine], normed.at[g, mine], gather_send.at[g, step],
                      gather_recv.at[g, mine], at_peer(target))

    def sibling_copy(g):
        return remote(normed.at[g, mine], normed.at[g, mine], gather_send.at[g, 0],
                      gather_recv.at[g, mine], at_peer(sibling))

    def forward_copy(g, step):
        slot = slot_of(lax.rem(chip + step, chips), core)
        return remote(normed.at[g, slot], normed.at[g, slot], forward_send.at[g, step],
                      gather_recv.at[g, slot], at_peer(sibling))

    def gather_arrival(g, slot):
        return remote(normed.at[g, slot], normed.at[g, slot], gather_send.at[g, 0],
                      gather_recv.at[g, slot], at_peer(sibling))

    half = width // HALVES

    def pair_copy(g, h):
        return remote(partial.at[g, h, pl.ds(other * chips, chips)], pair_in.at[g, h],
                      pair_send.at[g, h], pair_recv.at[g, h], at_peer(sibling))

    def return_copy(g, h, step):
        target = lax.rem(chip + step, chips)
        return remote(pair_out.at[g, h, target], returned.at[g, h, chip],
                      return_send.at[g, h, step], return_recv.at[g, h, chip],
                      at_peer(target * 2 + core))

    def return_arrival(g, h, origin):
        return remote(pair_out.at[g, h, origin], returned.at[g, h, origin],
                      return_send.at[g, h, 0], return_recv.at[g, h, origin], at_peer(sibling))

    def pass_copy(g, h):
        columns = pl.ds(h * half, half)
        return remote(out.at[g, :, columns], x_in.at[g, :, columns], pass_send.at[g, h],
                      pass_recv.at[g, h], at_section(lax.rem(section + 1, sections)))

    def enter(g):
        @pl.when(section == 0)
        def _():
            x_in[g, :, pl.ds(0, part)] = tokens[g]
            for origin in range(1, sections):
                token_copy(g, origin).wait_recv()

        @pl.when(section > 0)
        def _():
            for h in range(HALVES):
                pass_copy(g, h).wait_recv()

        wide = x_in[g].astype(jnp.float32)
        scale = lax.rsqrt(jnp.mean(wide * wide, axis=-1, keepdims=True) + EPS)
        normed[g, mine] = (wide * scale * gain[...]).astype(jnp.bfloat16)
        for step in range(1, chips):
            gather_copy(g, step).start()
        sibling_copy(g).start()

    def forward(g):
        for step in range(1, chips):
            gather_arrival(g, slot_of(lax.rem(chip + step, chips), core)).wait_recv()
            forward_copy(g, step).start()

    total_rows = peers * rows
    tile = 512 if hidden % 512 == 0 else hidden
    wide_lane = lax.broadcasted_iota(jnp.int32, (total_rows, LANES), 1)

    def project_in(g):
        for step in range(chips):
            gather_arrival(g, slot_of(lax.rem(chip + step, chips), other)).wait_recv()

        @pl.when(g == 0)
        def _():
            for copy in weight_copies(0) + weight_copies(1):
                copy.wait()
            for step in range(1, peers):
                origin = lax.rem(index + step, peers)
                slot = slot_of(lax.div(origin, 2), lax.rem(origin, 2))
                remote(shares.at[slot], shares.at[slot], share_send.at[step],
                       share_recv.at[slot], at_peer(origin)).wait_recv()

        every = shares[...].reshape(total_rows, LANES)
        factor = []
        for e in range(experts_local):
            pick = wide_lane == g * experts + index * experts_local + e
            factor.append(jnp.sum(jnp.where(pick, every, 0.0), axis=-1, keepdims=True))
        rows_in = normed[g].reshape(total_rows, width)
        for start in range(0, hidden, tile):
            if start == hidden // tile // 2 * tile:
                @pl.when(g > 0)
                def _():
                    for h in range(HALVES):
                        leave(g - 1, h)

            columns = pl.ds(start, tile)
            gate = jnp.dot(rows_in, w_gate[:, columns], preferred_element_type=jnp.float32)
            up = jnp.dot(rows_in, w_up[:, columns], preferred_element_type=jnp.float32)
            mid = gate / (1.0 + jnp.exp(-gate)) * up
            for begin in range(0, tile, LANES):
                piece = mid[:, begin:begin + LANES] * factor[(start + begin) // ff]
                active[:, pl.ds(start + begin, LANES)] = piece.astype(jnp.bfloat16)

    def project_out(g, h):
        if h == 0:
            @pl.when(g == 0)
            def _():
                for copy in weight_copies(2):
                    copy.wait()

        acts = active[...]
        result = jnp.dot(acts, w_down[:, pl.ds(h * half, half)],
                         preferred_element_type=jnp.float32)
        partial[g, h] = result.astype(jnp.bfloat16).reshape(peers, rows, half)
        pair_copy(g, h).start()

    def combine(g, h):
        pair_copy(g, h).wait_recv()
        for step in range(1, chips + 1):
            target = lax.rem(chip + step, chips)
            both = (partial[g, h, slot_of(target, core)].astype(jnp.float32)
                    + pair_in[g, h, target].astype(jnp.float32)).astype(jnp.bfloat16)
            pair_out[g, h, target] = both
            if step < chips:
                return_copy(g, h, step).start()

    def leave(g, h):
        columns = pl.ds(h * half, half)
        total = x_in[g, :, columns].astype(jnp.float32) + pair_out[g, h, chip].astype(jnp.float32)
        for step in range(1, chips):
            origin = lax.rem(chip + step, chips)
            return_arrival(g, h, origin).wait_recv()
            total += returned[g, h, origin].astype(jnp.float32)
        out[g, :, columns] = total.astype(jnp.bfloat16)

        @pl.when(section < sections - 1)
        def _():
            pass_copy(g, h).start()

    for step in range(1, peers):
        share_copy(step).start()

    enter(0)
    forward(0)

    def one(g, carry):
        project_in(g)

        @pl.when(g < groups - 1)
        def _():
            enter(g + 1)

        for h in range(HALVES):
            project_out(g, h)
        for h in range(HALVES):
            combine(g, h)

        @pl.when(g < groups - 1)
        def _():
            forward(g + 1)

        return carry

    lax.fori_loop(0, groups, one, 0)
    for h in range(HALVES):
        leave(groups - 1, h)

    for step in range(1, peers):
        share_copy(step).wait_send()

    def drain(g, carry):
        @pl.when(section > 0)
        def _():
            token_copy(g, section).wait_send()

        @pl.when(section < sections - 1)
        def _():
            for h in range(HALVES):
                pass_copy(g, h).wait_send()

        sibling_copy(g).wait_send()
        for step in range(1, chips):
            gather_copy(g, step).wait_send()
            forward_copy(g, step).wait_send()
        for h in range(HALVES):
            pair_copy(g, h).wait_send()
            for step in range(1, chips):
                return_copy(g, h, step).wait_send()
        return carry

    lax.fori_loop(0, groups, drain, 0)


def local(sections, peers, tokens, norm_gain, gate_weight, up_weight, down_weight, expert_ids,
          gate_probs):
    micro, rows_each, part = tokens.shape
    width = norm_gain.shape[1]
    groups, rows = micro // GROUP, rows_each * GROUP
    experts_local, ff = gate_weight.shape[1], gate_weight.shape[3]
    hidden = experts_local * ff
    top = expert_ids.shape[3]
    chips = peers // 2
    vmem = pl.BlockSpec(memory_space=pltpu.VMEM)
    anywhere = pl.BlockSpec(memory_space=pl.ANY)
    dma = pltpu.SemaphoreType.DMA
    bf16 = jnp.bfloat16
    result = pl.pallas_call(
        functools.partial(kernel, sections, peers, experts_local),
        out_shape=jax.ShapeDtypeStruct((groups, rows, width), bf16),
        in_specs=[vmem, vmem, anywhere, anywhere, anywhere, vmem, vmem],
        out_specs=vmem,
        scratch_shapes=[
            pltpu.VMEM((width, hidden), bf16),
            pltpu.VMEM((width, hidden), bf16),
            pltpu.VMEM((hidden, width), bf16),
            pltpu.VMEM((groups, rows, width), bf16),
            pltpu.VMEM((groups, peers, rows, width), bf16),
            pltpu.VMEM((peers * rows, hidden), bf16),
            pltpu.VMEM((groups, HALVES, peers, rows, width // HALVES), bf16),
            pltpu.VMEM((groups, HALVES, chips, rows, width // HALVES), bf16),
            pltpu.VMEM((groups, HALVES, chips, rows, width // HALVES), bf16),
            pltpu.VMEM((groups, HALVES, chips, rows, width // HALVES), bf16),
            pltpu.VMEM((peers, rows, LANES), jnp.float32),
            dma((3, experts_local)),
            dma((groups,)),
            dma((groups, sections)),
            dma((peers,)),
            dma((peers,)),
            dma((groups, chips)),
            dma((groups, peers)),
            dma((groups, chips)),
            dma((groups, HALVES)),
            dma((groups, HALVES)),
            dma((groups, HALVES, chips)),
            dma((groups, HALVES, chips)),
            dma((groups, HALVES)),
            dma((groups, HALVES)),
        ],
        compiler_params=pltpu.CompilerParams(
            collective_id=0, has_side_effects=True, vmem_limit_bytes=58 * 2**20
        ),
    )(
        tokens.reshape(groups, rows, part),
        norm_gain,
        gate_weight[0],
        up_weight[0],
        down_weight[0],
        expert_ids[0].reshape(groups, rows, top),
        gate_probs[0].reshape(groups, rows, top),
    )
    return result.reshape(1, micro, rows_each, width)


def solution(mesh):
    in_specs = (
        P(None, "expert", "section"),
        P("section", None),
        P("section", "expert", None, None),
        P("section", "expert", None, None),
        P("section", "expert", None, None),
        P("section", None, "expert", None),
        P("section", None, "expert", None),
    )
    out_specs = P("section", None, "expert", None)
    body = functools.partial(local, mesh.shape["section"], mesh.shape["expert"])
    return jax.shard_map(body, mesh=mesh, in_specs=in_specs, out_specs=out_specs, check_vma=False)
```

```python
import functools

import jax
import jax.numpy as jnp
from jax import lax
from jax.experimental import pallas as pl
from jax.experimental.pallas import tpu as pltpu
from jax.sharding import PartitionSpec as P

EPS = 1e-06
GROUP = 2
HALVES = 2
MESH = pl.DeviceIdType.MESH
LANES = 128


def kernel(
    sections, peers, experts_local,
    tokens, gain, gate_hbm, up_hbm, down_hbm, ids, probs,
    out,
    w_gate, w_up, w_down, x_in, normed, active, partial, pair_in, pair_out, returned, shares,
    weight_sem, token_send, token_recv, share_send, share_recv, gather_send, gather_recv,
    forward_send, pair_send, pair_recv, return_send, return_recv, pass_send, pass_recv,
):
    groups, rows, width = x_in.shape
    chips = peers // 2
    ff = gate_hbm.shape[2]
    hidden = experts_local * ff
    experts = experts_local * peers
    part = tokens.shape[2]
    section = lax.axis_index("section")
    index = lax.axis_index("expert")
    chip, core = lax.div(index, 2), lax.rem(index, 2)
    other = 1 - core
    sibling = chip * 2 + other

    def slot_of(chip_index, core_index):
        return core_index * chips + chip_index

    mine = slot_of(chip, core)

    def weight_copies(which):
        copies = []
        for e in range(experts_local):
            span = pl.ds(e * ff, ff)
            if which < 2:
                source, target = ((gate_hbm, w_gate), (up_hbm, w_up))[which]
                copies.append(pltpu.make_async_copy(
                    source.at[e], target.at[:, span], weight_sem.at[which, e]))
            else:
                copies.append(pltpu.make_async_copy(
                    down_hbm.at[e], w_down.at[span], weight_sem.at[which, e]))
        return copies

    for copy in weight_copies(0) + weight_copies(1) + weight_copies(2):
        copy.start()

    def remote(source, target, send, recv, device):
        return pltpu.make_async_remote_copy(
            src_ref=source, dst_ref=target, send_sem=send, recv_sem=recv,
            device_id=device, device_id_type=MESH)

    def at_peer(peer):
        return {"section": section, "expert": peer}

    def at_section(which):
        return {"section": which, "expert": index}

    barrier = pltpu.get_barrier_semaphore()
    for step in range(1, peers):
        pl.semaphore_signal(barrier, inc=1, device_id=at_peer(lax.rem(index + step, peers)),
                            device_id_type=MESH)
    for step in range(1, sections):
        pl.semaphore_signal(barrier, inc=1,
                            device_id=at_section(lax.rem(section + step, sections)),
                            device_id_type=MESH)
    pl.semaphore_wait(barrier, peers + sections - 2)

    def token_copy(g, origin):
        columns = pl.ds(pl.multiple_of(origin * part, part), part)
        return remote(tokens.at[g], x_in.at[g, :, columns], token_send.at[g],
                      token_recv.at[g, origin], at_section(0))

    @pl.when(section > 0)
    def _():
        for g in range(groups):
            token_copy(g, section).start()

    lane = lax.broadcasted_iota(jnp.int32, (rows, LANES), 1)
    spread = jnp.zeros((rows, LANES), jnp.float32)
    top = ids.shape[2]
    for g in range(groups):
        share = probs[g] / jnp.sum(probs[g], axis=-1, keepdims=True)
        named = ids[g] + g * experts
        for k in range(top):
            spread += jnp.where(named[:, k:k + 1] == lane, share[:, k:k + 1], 0.0)
    shares[mine] = spread

    def share_copy(step):
        target = lax.rem(index + step, peers)
        return remote(shares.at[mine], shares.at[mine], share_send.at[step],
                      share_recv.at[mine], at_peer(target))

    def gather_copy(g, step):
        target = lax.rem(chip + step, chips) * 2 + core
        return remote(normed.at[g, mine], normed.at[g, mine], gather_send.at[g, step],
                      gather_recv.at[g, mine], at_peer(target))

    def sibling_copy(g):
        return remote(normed.at[g, mine], normed.at[g, mine], gather_send.at[g, 0],
                      gather_recv.at[g, mine], at_peer(sibling))

    def forward_copy(g, step):
        slot = slot_of(lax.rem(chip + step, chips), core)
        return remote(normed.at[g, slot], normed.at[g, slot], forward_send.at[g, step],
                      gather_recv.at[g, slot], at_peer(sibling))

    def gather_arrival(g, slot):
        return remote(normed.at[g, slot], normed.at[g, slot], gather_send.at[g, 0],
                      gather_recv.at[g, slot], at_peer(sibling))

    half = width // HALVES

    def pair_copy(g, h):
        return remote(partial.at[g, h, pl.ds(other * chips, chips)], pair_in.at[g, h],
                      pair_send.at[g, h], pair_recv.at[g, h], at_peer(sibling))

    def return_copy(g, h, step):
        target = lax.rem(chip + step, chips)
        return remote(pair_out.at[g, h, target], returned.at[g, h, chip],
                      return_send.at[g, h, step], return_recv.at[g, h, chip],
                      at_peer(target * 2 + core))

    def return_arrival(g, h, origin):
        return remote(pair_out.at[g, h, origin], returned.at[g, h, origin],
                      return_send.at[g, h, 0], return_recv.at[g, h, origin], at_peer(sibling))

    def pass_copy(g, h):
        columns = pl.ds(h * half, half)
        return remote(out.at[g, :, columns], x_in.at[g, :, columns], pass_send.at[g, h],
                      pass_recv.at[g, h], at_section(lax.rem(section + 1, sections)))

    def enter(g):
        @pl.when(section == 0)
        def _():
            x_in[g, :, pl.ds(0, part)] = tokens[g]
            for origin in range(1, sections):
                token_copy(g, origin).wait_recv()

        @pl.when(section > 0)
        def _():
            for h in range(HALVES):
                pass_copy(g, h).wait_recv()

        wide = x_in[g].astype(jnp.float32)
        scale = lax.rsqrt(jnp.mean(wide * wide, axis=-1, keepdims=True) + EPS)
        normed[g, mine] = (wide * scale * gain[...]).astype(jnp.bfloat16)
        for step in range(1, chips):
            gather_copy(g, step).start()
        sibling_copy(g).start()

    def forward(g):
        for step in range(1, chips):
            gather_arrival(g, slot_of(lax.rem(chip + step, chips), core)).wait_recv()
            forward_copy(g, step).start()

    total_rows = peers * rows
    tile = 512 if hidden % 512 == 0 else hidden
    wide_lane = lax.broadcasted_iota(jnp.int32, (total_rows, LANES), 1)

    def project_in(g):
        for step in range(chips):
            gather_arrival(g, slot_of(lax.rem(chip + step, chips), other)).wait_recv()

        @pl.when(g == 0)
        def _():
            for copy in weight_copies(0) + weight_copies(1):
                copy.wait()
            for step in range(1, peers):
                origin = lax.rem(index + step, peers)
                slot = slot_of(lax.div(origin, 2), lax.rem(origin, 2))
                remote(shares.at[slot], shares.at[slot], share_send.at[step],
                       share_recv.at[slot], at_peer(origin)).wait_recv()

        every = shares[...].reshape(total_rows, LANES)
        factor = []
        for e in range(experts_local):
            pick = wide_lane == g * experts + index * experts_local + e
            factor.append(jnp.sum(jnp.where(pick, every, 0.0), axis=-1, keepdims=True))
        rows_in = normed[g].reshape(total_rows, width)
        for start in range(0, hidden, tile):
            if start == hidden // tile // 2 * tile:
                @pl.when(g > 0)
                def _():
                    for h in range(HALVES):
                        leave(g - 1, h)

            columns = pl.ds(start, tile)
            gate = jnp.dot(rows_in, w_gate[:, columns], preferred_element_type=jnp.float32)
            up = jnp.dot(rows_in, w_up[:, columns], preferred_element_type=jnp.float32)
            mid = gate / (1.0 + jnp.exp(-gate)) * up
            for begin in range(0, tile, LANES):
                piece = mid[:, begin:begin + LANES] * factor[(start + begin) // ff]
                active[:, pl.ds(start + begin, LANES)] = piece.astype(jnp.bfloat16)

    def project_out(g, h):
        if h == 0:
            @pl.when(g == 0)
            def _():
                for copy in weight_copies(2):
                    copy.wait()

        acts = active[...]
        result = jnp.dot(acts, w_down[:, pl.ds(h * half, half)],
                         preferred_element_type=jnp.float32)
        partial[g, h] = result.astype(jnp.bfloat16).reshape(peers, rows, half)
        pair_copy(g, h).start()

    def combine(g, h):
        pair_copy(g, h).wait_recv()
        for step in range(1, chips + 1):
            target = lax.rem(chip + step, chips)
            both = (partial[g, h, slot_of(target, core)].astype(jnp.float32)
                    + pair_in[g, h, target].astype(jnp.float32)).astype(jnp.bfloat16)
            pair_out[g, h, target] = both
            if step < chips:
                return_copy(g, h, step).start()

    def leave(g, h):
        columns = pl.ds(h * half, half)
        total = x_in[g, :, columns].astype(jnp.float32) + pair_out[g, h, chip].astype(jnp.float32)
        for step in range(1, chips):
            origin = lax.rem(chip + step, chips)
            return_arrival(g, h, origin).wait_recv()
            total += returned[g, h, origin].astype(jnp.float32)
        out[g, :, columns] = total.astype(jnp.bfloat16)

        @pl.when(section < sections - 1)
        def _():
            pass_copy(g, h).start()

    for step in range(1, peers):
        share_copy(step).start()

    enter(0)
    ahead = jnp.where(section == 0, 2, 1)

    @pl.when(section == 0)
    def _():
        enter(1)

    forward(0)

    def one(g, carry):
        project_in(g)

        @pl.when(g + ahead < groups)
        def _():
            enter(g + ahead)

        for h in range(HALVES):
            project_out(g, h)
        for h in range(HALVES - 1):
            combine(g, h)

        @pl.when(g < groups - 1)
        def _():
            forward(g + 1)

        combine(g, HALVES - 1)

        return carry

    lax.fori_loop(0, groups, one, 0)
    for h in range(HALVES):
        leave(groups - 1, h)

    for step in range(1, peers):
        share_copy(step).wait_send()

    def drain(g, carry):
        @pl.when(section > 0)
        def _():
            token_copy(g, section).wait_send()

        @pl.when(section < sections - 1)
        def _():
            for h in range(HALVES):
                pass_copy(g, h).wait_send()

        sibling_copy(g).wait_send()
        for step in range(1, chips):
            gather_copy(g, step).wait_send()
            forward_copy(g, step).wait_send()
        for h in range(HALVES):
            pair_copy(g, h).wait_send()
            for step in range(1, chips):
                return_copy(g, h, step).wait_send()
        return carry

    lax.fori_loop(0, groups, drain, 0)


def local(sections, peers, tokens, norm_gain, gate_weight, up_weight, down_weight, expert_ids,
          gate_probs):
    micro, rows_each, part = tokens.shape
    width = norm_gain.shape[1]
    groups, rows = micro // GROUP, rows_each * GROUP
    experts_local, ff = gate_weight.shape[1], gate_weight.shape[3]
    hidden = experts_local * ff
    top = expert_ids.shape[3]
    chips = peers // 2
    vmem = pl.BlockSpec(memory_space=pltpu.VMEM)
    anywhere = pl.BlockSpec(memory_space=pl.ANY)
    dma = pltpu.SemaphoreType.DMA
    bf16 = jnp.bfloat16
    result = pl.pallas_call(
        functools.partial(kernel, sections, peers, experts_local),
        out_shape=jax.ShapeDtypeStruct((groups, rows, width), bf16),
        in_specs=[vmem, vmem, anywhere, anywhere, anywhere, vmem, vmem],
        out_specs=vmem,
        scratch_shapes=[
            pltpu.VMEM((width, hidden), bf16),
            pltpu.VMEM((width, hidden), bf16),
            pltpu.VMEM((hidden, width), bf16),
            pltpu.VMEM((groups, rows, width), bf16),
            pltpu.VMEM((groups, peers, rows, width), bf16),
            pltpu.VMEM((peers * rows, hidden), bf16),
            pltpu.VMEM((groups, HALVES, peers, rows, width // HALVES), bf16),
            pltpu.VMEM((groups, HALVES, chips, rows, width // HALVES), bf16),
            pltpu.VMEM((groups, HALVES, chips, rows, width // HALVES), bf16),
            pltpu.VMEM((groups, HALVES, chips, rows, width // HALVES), bf16),
            pltpu.VMEM((peers, rows, LANES), jnp.float32),
            dma((3, experts_local)),
            dma((groups,)),
            dma((groups, sections)),
            dma((peers,)),
            dma((peers,)),
            dma((groups, chips)),
            dma((groups, peers)),
            dma((groups, chips)),
            dma((groups, HALVES)),
            dma((groups, HALVES)),
            dma((groups, HALVES, chips)),
            dma((groups, HALVES, chips)),
            dma((groups, HALVES)),
            dma((groups, HALVES)),
        ],
        compiler_params=pltpu.CompilerParams(
            collective_id=0, has_side_effects=True, vmem_limit_bytes=58 * 2**20
        ),
    )(
        tokens.reshape(groups, rows, part),
        norm_gain,
        gate_weight[0],
        up_weight[0],
        down_weight[0],
        expert_ids[0].reshape(groups, rows, top),
        gate_probs[0].reshape(groups, rows, top),
    )
    return result.reshape(1, micro, rows_each, width)


def solution(mesh):
    in_specs = (
        P(None, "expert", "section"),
        P("section", None),
        P("section", "expert", None, None),
        P("section", "expert", None, None),
        P("section", "expert", None, None),
        P("section", None, "expert", None),
        P("section", None, "expert", None),
    )
    out_specs = P("section", None, "expert", None)
    body = functools.partial(local, mesh.shape["section"], mesh.shape["expert"])
    return jax.shard_map(body, mesh=mesh, in_specs=in_specs, out_specs=out_specs, check_vma=False)
```

```python
import functools

import jax
import jax.numpy as jnp
from jax import lax
from jax.experimental import pallas as pl
from jax.experimental.pallas import tpu as pltpu
from jax.sharding import PartitionSpec as P

EPS = 1e-06
GROUP = 4
HALVES = 2
MESH = pl.DeviceIdType.MESH
LANES = 128


def kernel(
    sections, peers, experts_local,
    tokens, gain, gate_hbm, up_hbm, down_hbm, ids, probs,
    out,
    w_gate, w_up, w_down, x_in, normed, active, partial, pair_in, pair_out, returned, shares,
    weight_sem, token_send, token_recv, share_send, share_recv, gather_send, gather_recv,
    forward_send, pair_send, pair_recv, return_send, return_recv, pass_send, pass_recv,
):
    groups, rows, width = x_in.shape
    chips = peers // 2
    ff = gate_hbm.shape[2]
    hidden = experts_local * ff
    experts = experts_local * peers
    part = tokens.shape[2]
    section = lax.axis_index("section")
    index = lax.axis_index("expert")
    chip, core = lax.div(index, 2), lax.rem(index, 2)
    other = 1 - core
    sibling = chip * 2 + other

    def slot_of(chip_index, core_index):
        return core_index * chips + chip_index

    mine = slot_of(chip, core)

    def weight_copies(which):
        copies = []
        for e in range(experts_local):
            span = pl.ds(e * ff, ff)
            if which < 2:
                source, target = ((gate_hbm, w_gate), (up_hbm, w_up))[which]
                copies.append(pltpu.make_async_copy(
                    source.at[e], target.at[:, span], weight_sem.at[which, e]))
            else:
                copies.append(pltpu.make_async_copy(
                    down_hbm.at[e], w_down.at[span], weight_sem.at[which, e]))
        return copies

    for copy in weight_copies(0) + weight_copies(1) + weight_copies(2):
        copy.start()

    def remote(source, target, send, recv, device):
        return pltpu.make_async_remote_copy(
            src_ref=source, dst_ref=target, send_sem=send, recv_sem=recv,
            device_id=device, device_id_type=MESH)

    def at_peer(peer):
        return {"section": section, "expert": peer}

    def at_section(which):
        return {"section": which, "expert": index}

    barrier = pltpu.get_barrier_semaphore()
    for step in range(1, peers):
        pl.semaphore_signal(barrier, inc=1, device_id=at_peer(lax.rem(index + step, peers)),
                            device_id_type=MESH)
    for step in range(1, sections):
        pl.semaphore_signal(barrier, inc=1,
                            device_id=at_section(lax.rem(section + step, sections)),
                            device_id_type=MESH)
    pl.semaphore_wait(barrier, peers + sections - 2)

    def token_copy(g, origin):
        columns = pl.ds(pl.multiple_of(origin * part, part), part)
        return remote(tokens.at[g], x_in.at[g, :, columns], token_send.at[g],
                      token_recv.at[g, origin], at_section(0))

    @pl.when(section > 0)
    def _():
        for g in range(groups):
            token_copy(g, section).start()

    lane = lax.broadcasted_iota(jnp.int32, (rows, LANES), 1)
    spread = jnp.zeros((rows, LANES), jnp.float32)
    top = ids.shape[2]
    for g in range(groups):
        share = probs[g] / jnp.sum(probs[g], axis=-1, keepdims=True)
        named = ids[g] + g * experts
        for k in range(top):
            spread += jnp.where(named[:, k:k + 1] == lane, share[:, k:k + 1], 0.0)
    shares[mine] = spread

    def share_copy(step):
        target = lax.rem(index + step, peers)
        return remote(shares.at[mine], shares.at[mine], share_send.at[step],
                      share_recv.at[mine], at_peer(target))

    def gather_copy(g, step):
        target = lax.rem(chip + step, chips) * 2 + core
        return remote(normed.at[g, mine], normed.at[g, mine], gather_send.at[g, step],
                      gather_recv.at[g, mine], at_peer(target))

    def sibling_copy(g):
        return remote(normed.at[g, mine], normed.at[g, mine], gather_send.at[g, 0],
                      gather_recv.at[g, mine], at_peer(sibling))

    def forward_copy(g, step):
        slot = slot_of(lax.rem(chip + step, chips), core)
        return remote(normed.at[g, slot], normed.at[g, slot], forward_send.at[g, step],
                      gather_recv.at[g, slot], at_peer(sibling))

    def gather_arrival(g, slot):
        return remote(normed.at[g, slot], normed.at[g, slot], gather_send.at[g, 0],
                      gather_recv.at[g, slot], at_peer(sibling))

    half = width // HALVES

    def pair_copy(g, h):
        return remote(partial.at[g, h, pl.ds(other * chips, chips)], pair_in.at[g, h],
                      pair_send.at[g, h], pair_recv.at[g, h], at_peer(sibling))

    def return_copy(g, h, step):
        target = lax.rem(chip + step, chips)
        return remote(pair_out.at[g, h, target], returned.at[g, h, chip],
                      return_send.at[g, h, step], return_recv.at[g, h, chip],
                      at_peer(target * 2 + core))

    def return_arrival(g, h, origin):
        return remote(pair_out.at[g, h, origin], returned.at[g, h, origin],
                      return_send.at[g, h, 0], return_recv.at[g, h, origin], at_peer(sibling))

    def pass_copy(g, h):
        columns = pl.ds(h * half, half)
        return remote(out.at[g, :, columns], x_in.at[g, :, columns], pass_send.at[g, h],
                      pass_recv.at[g, h], at_section(lax.rem(section + 1, sections)))

    def enter(g):
        @pl.when(section == 0)
        def _():
            x_in[g, :, pl.ds(0, part)] = tokens[g]
            for origin in range(1, sections):
                token_copy(g, origin).wait_recv()

        @pl.when(section > 0)
        def _():
            for h in range(HALVES):
                pass_copy(g, h).wait_recv()

        wide = x_in[g].astype(jnp.float32)
        scale = lax.rsqrt(jnp.mean(wide * wide, axis=-1, keepdims=True) + EPS)
        normed[g, mine] = (wide * scale * gain[...]).astype(jnp.bfloat16)
        for step in range(1, chips):
            gather_copy(g, step).start()
        sibling_copy(g).start()

    def forward(g):
        for step in range(1, chips):
            gather_arrival(g, slot_of(lax.rem(chip + step, chips), core)).wait_recv()
            forward_copy(g, step).start()

    total_rows = peers * rows
    tile = 512 if hidden % 512 == 0 else hidden
    wide_lane = lax.broadcasted_iota(jnp.int32, (total_rows, LANES), 1)

    def project_in(g):
        for step in range(chips):
            gather_arrival(g, slot_of(lax.rem(chip + step, chips), other)).wait_recv()

        @pl.when(g == 0)
        def _():
            for copy in weight_copies(0) + weight_copies(1):
                copy.wait()
            for step in range(1, peers):
                origin = lax.rem(index + step, peers)
                slot = slot_of(lax.div(origin, 2), lax.rem(origin, 2))
                remote(shares.at[slot], shares.at[slot], share_send.at[step],
                       share_recv.at[slot], at_peer(origin)).wait_recv()

        every = shares[...].reshape(total_rows, LANES)
        factor = []
        for e in range(experts_local):
            pick = wide_lane == g * experts + index * experts_local + e
            factor.append(jnp.sum(jnp.where(pick, every, 0.0), axis=-1, keepdims=True))
        rows_in = normed[g].reshape(total_rows, width)
        for start in range(0, hidden, tile):
            if start == hidden // tile // 2 * tile:
                @pl.when(g > 0)
                def _():
                    for h in range(HALVES):
                        leave(g - 1, h)

            columns = pl.ds(start, tile)
            gate = jnp.dot(rows_in, w_gate[:, columns], preferred_element_type=jnp.float32)
            up = jnp.dot(rows_in, w_up[:, columns], preferred_element_type=jnp.float32)
            mid = gate / (1.0 + jnp.exp(-gate)) * up
            for begin in range(0, tile, LANES):
                piece = mid[:, begin:begin + LANES] * factor[(start + begin) // ff]
                active[:, pl.ds(start + begin, LANES)] = piece.astype(jnp.bfloat16)

    def project_out(g, h):
        if h == 0:
            @pl.when(g == 0)
            def _():
                for copy in weight_copies(2):
                    copy.wait()

        acts = active[...]
        result = jnp.dot(acts, w_down[:, pl.ds(h * half, half)],
                         preferred_element_type=jnp.float32)
        partial[g, h] = result.astype(jnp.bfloat16).reshape(peers, rows, half)
        pair_copy(g, h).start()

    def combine(g, h):
        pair_copy(g, h).wait_recv()
        for step in range(1, chips + 1):
            target = lax.rem(chip + step, chips)
            both = (partial[g, h, slot_of(target, core)].astype(jnp.float32)
                    + pair_in[g, h, target].astype(jnp.float32)).astype(jnp.bfloat16)
            pair_out[g, h, target] = both
            if step < chips:
                return_copy(g, h, step).start()

    def leave(g, h):
        columns = pl.ds(h * half, half)
        total = x_in[g, :, columns].astype(jnp.float32) + pair_out[g, h, chip].astype(jnp.float32)
        for step in range(1, chips):
            origin = lax.rem(chip + step, chips)
            return_arrival(g, h, origin).wait_recv()
            total += returned[g, h, origin].astype(jnp.float32)
        out[g, :, columns] = total.astype(jnp.bfloat16)

        @pl.when(section < sections - 1)
        def _():
            pass_copy(g, h).start()

    for step in range(1, peers):
        share_copy(step).start()

    enter(0)
    ahead = jnp.where(section == 0, 2, 1)

    @pl.when(section == 0)
    def _():
        enter(1)

    forward(0)

    def one(g, carry):
        project_in(g)

        @pl.when(g + ahead < groups)
        def _():
            enter(g + ahead)

        for h in range(HALVES):
            project_out(g, h)
        for h in range(HALVES - 1):
            combine(g, h)

        @pl.when(g < groups - 1)
        def _():
            forward(g + 1)

        combine(g, HALVES - 1)

        return carry

    lax.fori_loop(0, groups, one, 0)
    for h in range(HALVES):
        leave(groups - 1, h)

    for step in range(1, peers):
        share_copy(step).wait_send()

    def drain(g, carry):
        @pl.when(section > 0)
        def _():
            token_copy(g, section).wait_send()

        @pl.when(section < sections - 1)
        def _():
            for h in range(HALVES):
                pass_copy(g, h).wait_send()

        sibling_copy(g).wait_send()
        for step in range(1, chips):
            gather_copy(g, step).wait_send()
            forward_copy(g, step).wait_send()
        for h in range(HALVES):
            pair_copy(g, h).wait_send()
            for step in range(1, chips):
                return_copy(g, h, step).wait_send()
        return carry

    lax.fori_loop(0, groups, drain, 0)


def local(sections, peers, tokens, norm_gain, gate_weight, up_weight, down_weight, expert_ids,
          gate_probs):
    micro, rows_each, part = tokens.shape
    width = norm_gain.shape[1]
    groups, rows = micro // GROUP, rows_each * GROUP
    experts_local, ff = gate_weight.shape[1], gate_weight.shape[3]
    hidden = experts_local * ff
    top = expert_ids.shape[3]
    chips = peers // 2
    vmem = pl.BlockSpec(memory_space=pltpu.VMEM)
    anywhere = pl.BlockSpec(memory_space=pl.ANY)
    dma = pltpu.SemaphoreType.DMA
    bf16 = jnp.bfloat16
    result = pl.pallas_call(
        functools.partial(kernel, sections, peers, experts_local),
        out_shape=jax.ShapeDtypeStruct((groups, rows, width), bf16),
        in_specs=[vmem, vmem, anywhere, anywhere, anywhere, vmem, vmem],
        out_specs=vmem,
        scratch_shapes=[
            pltpu.VMEM((width, hidden), bf16),
            pltpu.VMEM((width, hidden), bf16),
            pltpu.VMEM((hidden, width), bf16),
            pltpu.VMEM((groups, rows, width), bf16),
            pltpu.VMEM((groups, peers, rows, width), bf16),
            pltpu.VMEM((peers * rows, hidden), bf16),
            pltpu.VMEM((groups, HALVES, peers, rows, width // HALVES), bf16),
            pltpu.VMEM((groups, HALVES, chips, rows, width // HALVES), bf16),
            pltpu.VMEM((groups, HALVES, chips, rows, width // HALVES), bf16),
            pltpu.VMEM((groups, HALVES, chips, rows, width // HALVES), bf16),
            pltpu.VMEM((peers, rows, LANES), jnp.float32),
            dma((3, experts_local)),
            dma((groups,)),
            dma((groups, sections)),
            dma((peers,)),
            dma((peers,)),
            dma((groups, chips)),
            dma((groups, peers)),
            dma((groups, chips)),
            dma((groups, HALVES)),
            dma((groups, HALVES)),
            dma((groups, HALVES, chips)),
            dma((groups, HALVES, chips)),
            dma((groups, HALVES)),
            dma((groups, HALVES)),
        ],
        compiler_params=pltpu.CompilerParams(
            collective_id=0, has_side_effects=True, vmem_limit_bytes=58 * 2**20
        ),
    )(
        tokens.reshape(groups, rows, part),
        norm_gain,
        gate_weight[0],
        up_weight[0],
        down_weight[0],
        expert_ids[0].reshape(groups, rows, top),
        gate_probs[0].reshape(groups, rows, top),
    )
    return result.reshape(1, micro, rows_each, width)


def solution(mesh):
    in_specs = (
        P(None, "expert", "section"),
        P("section", None),
        P("section", "expert", None, None),
        P("section", "expert", None, None),
        P("section", "expert", None, None),
        P("section", None, "expert", None),
        P("section", None, "expert", None),
    )
    out_specs = P("section", None, "expert", None)
    body = functools.partial(local, mesh.shape["section"], mesh.shape["expert"])
    return jax.shard_map(body, mesh=mesh, in_specs=in_specs, out_specs=out_specs, check_vma=False)
```

```python
import functools

import jax
import jax.numpy as jnp
from jax import lax
from jax.experimental import pallas as pl
from jax.experimental.pallas import tpu as pltpu
from jax.sharding import PartitionSpec as P

EPS = 1e-06
GROUP = 2
CAP = 2
BLOCK = 8
HALVES = 2
MESH = pl.DeviceIdType.MESH
LANES = 128


def kernel(
    sections, peers, experts_local,
    tokens, gain, gate_hbm, up_hbm, down_hbm, ids, probs,
    out,
    w_in, w_down, x_in, normed, active, chosen, partial, pair_in, pair_out, returned, shares,
    weight_sem, token_send, token_recv, share_send, share_recv, gather_send, gather_recv,
    forward_send, pair_send, pair_recv, return_send, return_recv, pass_send, pass_recv,
):
    groups, rows, width = x_in.shape
    chips = peers // 2
    ff = gate_hbm.shape[2]
    hidden = experts_local * ff
    experts = experts_local * peers
    part = tokens.shape[2]
    section = lax.axis_index("section")
    index = lax.axis_index("expert")
    chip, core = lax.div(index, 2), lax.rem(index, 2)
    other = 1 - core
    sibling = chip * 2 + other

    def slot_of(chip_index, core_index):
        return core_index * chips + chip_index

    mine = slot_of(chip, core)

    def weight_copies(which):
        copies = []
        for e in range(experts_local):
            if which < 2:
                source = (gate_hbm, up_hbm)[which]
                copies.append(pltpu.make_async_copy(
                    source.at[e], w_in.at[:, pl.ds((2 * e + which) * ff, ff)],
                    weight_sem.at[which, e]))
            else:
                copies.append(pltpu.make_async_copy(
                    down_hbm.at[e], w_down.at[pl.ds(e * ff, ff)], weight_sem.at[which, e]))
        return copies

    for copy in weight_copies(0) + weight_copies(1) + weight_copies(2):
        copy.start()

    def remote(source, target, send, recv, device):
        return pltpu.make_async_remote_copy(
            src_ref=source, dst_ref=target, send_sem=send, recv_sem=recv,
            device_id=device, device_id_type=MESH)

    def at_peer(peer):
        return {"section": section, "expert": peer}

    def at_section(which):
        return {"section": which, "expert": index}

    barrier = pltpu.get_barrier_semaphore()
    for step in range(1, peers):
        pl.semaphore_signal(barrier, inc=1, device_id=at_peer(lax.rem(index + step, peers)),
                            device_id_type=MESH)
    for step in range(1, sections):
        pl.semaphore_signal(barrier, inc=1,
                            device_id=at_section(lax.rem(section + step, sections)),
                            device_id_type=MESH)
    pl.semaphore_wait(barrier, peers + sections - 2)

    def token_copy(g, origin):
        columns = pl.ds(pl.multiple_of(origin * part, part), part)
        return remote(tokens.at[g], x_in.at[g, :, columns], token_send.at[g],
                      token_recv.at[g, origin], at_section(0))

    @pl.when(section > 0)
    def _():
        for g in range(groups):
            token_copy(g, section).start()

    lane = lax.broadcasted_iota(jnp.int32, (rows, LANES), 1)
    spread = jnp.zeros((rows, LANES), jnp.float32)
    top = ids.shape[2]
    for g in range(groups):
        share = probs[g] / jnp.sum(probs[g], axis=-1, keepdims=True)
        named = ids[g] + g * experts
        for k in range(top):
            spread += jnp.where(named[:, k:k + 1] == lane, share[:, k:k + 1], 0.0)
    shares[mine] = spread

    def share_copy(step):
        target = lax.rem(index + step, peers)
        return remote(shares.at[mine], shares.at[mine], share_send.at[step],
                      share_recv.at[mine], at_peer(target))

    def gather_copy(g, step):
        target = lax.rem(chip + step, chips) * 2 + core
        return remote(normed.at[g, mine], normed.at[g, mine], gather_send.at[g, step],
                      gather_recv.at[g, mine], at_peer(target))

    def sibling_copy(g):
        return remote(normed.at[g, mine], normed.at[g, mine], gather_send.at[g, 0],
                      gather_recv.at[g, mine], at_peer(sibling))

    def forward_copy(g, step):
        slot = slot_of(lax.rem(chip + step, chips), core)
        return remote(normed.at[g, slot], normed.at[g, slot], forward_send.at[g, step],
                      gather_recv.at[g, slot], at_peer(sibling))

    def gather_arrival(g, slot):
        return remote(normed.at[g, slot], normed.at[g, slot], gather_send.at[g, 0],
                      gather_recv.at[g, slot], at_peer(sibling))

    half = width // HALVES

    def pair_copy(g, h):
        return remote(partial.at[g, h, pl.ds(other * chips, chips)], pair_in.at[g, h],
                      pair_send.at[g, h], pair_recv.at[g, h], at_peer(sibling))

    def return_copy(g, h, step):
        target = lax.rem(chip + step, chips)
        return remote(pair_out.at[g, h, target], returned.at[g, h, chip],
                      return_send.at[g, h, step], return_recv.at[g, h, chip],
                      at_peer(target * 2 + core))

    def return_arrival(g, h, origin):
        return remote(pair_out.at[g, h, origin], returned.at[g, h, origin],
                      return_send.at[g, h, 0], return_recv.at[g, h, origin], at_peer(sibling))

    def pass_copy(g, h):
        columns = pl.ds(h * half, half)
        return remote(out.at[g, :, columns], x_in.at[g, :, columns], pass_send.at[g, h],
                      pass_recv.at[g, h], at_section(lax.rem(section + 1, sections)))

    def enter(g):
        @pl.when(section == 0)
        def _():
            x_in[g, :, pl.ds(0, part)] = tokens[g]
            for origin in range(1, sections):
                token_copy(g, origin).wait_recv()

        @pl.when(section > 0)
        def _():
            for h in range(HALVES):
                pass_copy(g, h).wait_recv()

        wide = x_in[g].astype(jnp.float32)
        scale = lax.rsqrt(jnp.mean(wide * wide, axis=-1, keepdims=True) + EPS)
        normed[g, mine] = (wide * scale * gain[...]).astype(jnp.bfloat16)
        for step in range(1, chips):
            gather_copy(g, step).start()
        sibling_copy(g).start()

    def forward(g):
        for step in range(1, chips):
            gather_arrival(g, slot_of(lax.rem(chip + step, chips), core)).wait_recv()
            forward_copy(g, step).start()

    total_rows = peers * rows
    slots = CAP * (total_rows // BLOCK)
    all_slots = experts_local * slots
    wide_lane = lax.broadcasted_iota(jnp.int32, (total_rows, LANES), 1)
    slot_lane = lax.broadcasted_iota(jnp.int32, (total_rows, all_slots), 1).astype(jnp.float32)

    def project_in(g):
        @pl.when(g == 0)
        def _():
            for step in range(1, peers):
                origin = lax.rem(index + step, peers)
                slot = slot_of(lax.div(origin, 2), lax.rem(origin, 2))
                remote(shares.at[slot], shares.at[slot], share_send.at[step],
                       share_recv.at[slot], at_peer(origin)).wait_recv()

        every = shares[...].reshape(total_rows, LANES)
        below = (lax.broadcasted_iota(jnp.int32, (total_rows, total_rows), 0)
                 > lax.broadcasted_iota(jnp.int32, (total_rows, total_rows), 1))
        ranks = jnp.dot(jnp.where(below, 1.0, 0.0).astype(jnp.bfloat16),
                        jnp.where(every > 0.0, 1.0, 0.0).astype(jnp.bfloat16),
                        preferred_element_type=jnp.float32)
        weighted = jnp.zeros((total_rows, all_slots), jnp.float32)
        for e in range(experts_local):
            pick = wide_lane == g * experts + index * experts_local + e
            factor = jnp.sum(jnp.where(pick, every, 0.0), axis=-1, keepdims=True)
            rank = jnp.sum(jnp.where(pick, ranks, 0.0), axis=-1, keepdims=True)
            inside = (slot_lane >= e * slots) & (slot_lane < (e + 1) * slots)
            weighted += jnp.where(inside & (rank + e * slots == slot_lane), factor, 0.0)
        chosen[...] = jnp.where(weighted > 0.0, 1.0, 0.0).astype(jnp.bfloat16)
        flipped = weighted.T
        slot_share = jnp.sum(flipped, axis=-1, keepdims=True)
        picker = jnp.where(flipped > 0.0, 1.0, 0.0).astype(jnp.bfloat16)

        for step in range(chips):
            gather_arrival(g, slot_of(lax.rem(chip + step, chips), other)).wait_recv()

        @pl.when(g == 0)
        def _():
            for copy in weight_copies(0) + weight_copies(1):
                copy.wait()

        rows_in = jnp.dot(picker, normed[g].reshape(total_rows, width),
                          preferred_element_type=jnp.float32).astype(jnp.bfloat16)
        for e in range(experts_local):
            if e == experts_local // 2:
                @pl.when(g > 0)
                def _():
                    for h in range(HALVES):
                        leave(g - 1, h)

            span = slice(e * slots, (e + 1) * slots)
            both = jnp.dot(rows_in[span], w_in[:, pl.ds(2 * e * ff, 2 * ff)],
                           preferred_element_type=jnp.float32)
            gate, up = both[:, :ff], both[:, ff:]
            mid = gate / (1.0 + jnp.exp(-gate)) * up * slot_share[span]
            active[e] = mid.astype(jnp.bfloat16)

    def project_out(g, h):
        if h == 0:
            @pl.when(g == 0)
            def _():
                for copy in weight_copies(2):
                    copy.wait()

        columns = pl.ds(h * half, half)
        pieces = [
            jnp.dot(active[e], w_down[pl.ds(e * ff, ff), columns],
                    preferred_element_type=jnp.float32).astype(jnp.bfloat16)
            for e in range(experts_local)
        ]
        result = jnp.dot(chosen[...], jnp.concatenate(pieces, axis=0),
                         preferred_element_type=jnp.float32)
        partial[g, h] = result.astype(jnp.bfloat16).reshape(peers, rows, half)
        pair_copy(g, h).start()

    def combine(g, h):
        pair_copy(g, h).wait_recv()
        for step in range(1, chips + 1):
            target = lax.rem(chip + step, chips)
            both = (partial[g, h, slot_of(target, core)].astype(jnp.float32)
                    + pair_in[g, h, target].astype(jnp.float32)).astype(jnp.bfloat16)
            pair_out[g, h, target] = both
            if step < chips:
                return_copy(g, h, step).start()

    def leave(g, h):
        columns = pl.ds(h * half, half)
        total = x_in[g, :, columns].astype(jnp.float32) + pair_out[g, h, chip].astype(jnp.float32)
        for step in range(1, chips):
            origin = lax.rem(chip + step, chips)
            return_arrival(g, h, origin).wait_recv()
            total += returned[g, h, origin].astype(jnp.float32)
        out[g, :, columns] = total.astype(jnp.bfloat16)

        @pl.when(section < sections - 1)
        def _():
            pass_copy(g, h).start()

    for step in range(1, peers):
        share_copy(step).start()

    enter(0)
    ahead = jnp.where(section == 0, 2, 1)

    @pl.when(section == 0)
    def _():
        enter(1)

    forward(0)

    def one(g, carry):
        project_in(g)

        @pl.when(g + ahead < groups)
        def _():
            enter(g + ahead)

        for h in range(HALVES):
            project_out(g, h)
        for h in range(HALVES - 1):
            combine(g, h)

        @pl.when(g < groups - 1)
        def _():
            forward(g + 1)

        combine(g, HALVES - 1)

        return carry

    lax.fori_loop(0, groups, one, 0)
    for h in range(HALVES):
        leave(groups - 1, h)

    for step in range(1, peers):
        share_copy(step).wait_send()

    def drain(g, carry):
        @pl.when(section > 0)
        def _():
            token_copy(g, section).wait_send()

        @pl.when(section < sections - 1)
        def _():
            for h in range(HALVES):
                pass_copy(g, h).wait_send()

        sibling_copy(g).wait_send()
        for step in range(1, chips):
            gather_copy(g, step).wait_send()
            forward_copy(g, step).wait_send()
        for h in range(HALVES):
            pair_copy(g, h).wait_send()
            for step in range(1, chips):
                return_copy(g, h, step).wait_send()
        return carry

    lax.fori_loop(0, groups, drain, 0)


def local(sections, peers, tokens, norm_gain, gate_weight, up_weight, down_weight, expert_ids,
          gate_probs):
    micro, rows_each, part = tokens.shape
    width = norm_gain.shape[1]
    groups, rows = micro // GROUP, rows_each * GROUP
    experts_local, ff = gate_weight.shape[1], gate_weight.shape[3]
    hidden = experts_local * ff
    top = expert_ids.shape[3]
    chips = peers // 2
    slots = CAP * (peers * rows // BLOCK)
    vmem = pl.BlockSpec(memory_space=pltpu.VMEM)
    anywhere = pl.BlockSpec(memory_space=pl.ANY)
    dma = pltpu.SemaphoreType.DMA
    bf16 = jnp.bfloat16
    result = pl.pallas_call(
        functools.partial(kernel, sections, peers, experts_local),
        out_shape=jax.ShapeDtypeStruct((groups, rows, width), bf16),
        in_specs=[vmem, vmem, anywhere, anywhere, anywhere, vmem, vmem],
        out_specs=vmem,
        scratch_shapes=[
            pltpu.VMEM((width, 2 * hidden), bf16),
            pltpu.VMEM((hidden, width), bf16),
            pltpu.VMEM((groups, rows, width), bf16),
            pltpu.VMEM((groups, peers, rows, width), bf16),
            pltpu.VMEM((experts_local, slots, ff), bf16),
            pltpu.VMEM((peers * rows, experts_local * slots), bf16),
            pltpu.VMEM((groups, HALVES, peers, rows, width // HALVES), bf16),
            pltpu.VMEM((groups, HALVES, chips, rows, width // HALVES), bf16),
            pltpu.VMEM((groups, HALVES, chips, rows, width // HALVES), bf16),
            pltpu.VMEM((groups, HALVES, chips, rows, width // HALVES), bf16),
            pltpu.VMEM((peers, rows, LANES), jnp.float32),
            dma((3, experts_local)),
            dma((groups,)),
            dma((groups, sections)),
            dma((peers,)),
            dma((peers,)),
            dma((groups, chips)),
            dma((groups, peers)),
            dma((groups, chips)),
            dma((groups, HALVES)),
            dma((groups, HALVES)),
            dma((groups, HALVES, chips)),
            dma((groups, HALVES, chips)),
            dma((groups, HALVES)),
            dma((groups, HALVES)),
        ],
        compiler_params=pltpu.CompilerParams(
            collective_id=0, has_side_effects=True, vmem_limit_bytes=58 * 2**20
        ),
    )(
        tokens.reshape(groups, rows, part),
        norm_gain,
        gate_weight[0],
        up_weight[0],
        down_weight[0],
        expert_ids[0].reshape(groups, rows, top),
        gate_probs[0].reshape(groups, rows, top),
    )
    return result.reshape(1, micro, rows_each, width)


def solution(mesh):
    in_specs = (
        P(None, "expert", "section"),
        P("section", None),
        P("section", "expert", None, None),
        P("section", "expert", None, None),
        P("section", "expert", None, None),
        P("section", None, "expert", None),
        P("section", None, "expert", None),
    )
    out_specs = P("section", None, "expert", None)
    body = functools.partial(local, mesh.shape["section"], mesh.shape["expert"])
    return jax.shard_map(body, mesh=mesh, in_specs=in_specs, out_specs=out_specs, check_vma=False)
```

```python
import functools

import jax
import jax.numpy as jnp
from jax import lax
from jax.experimental import pallas as pl
from jax.experimental.pallas import tpu as pltpu
from jax.sharding import PartitionSpec as P

EPS = 1e-06
GROUP = 2
CAP = 2
BLOCK = 8
HALVES = 2
MESH = pl.DeviceIdType.MESH
LANES = 128


def kernel(
    sections, peers, experts_local,
    tokens, gain, gate_hbm, up_hbm, down_hbm, ids, probs,
    out,
    w_in, w_down, x_in, normed, active, chosen, partial, pair_in, pair_out, returned, shares,
    weight_sem, token_send, token_recv, share_send, share_recv, gather_send, gather_recv,
    forward_send, pair_send, pair_recv, return_send, return_recv, pass_send, pass_recv,
):
    groups, rows, width = x_in.shape
    chips = peers // 2
    ff = gate_hbm.shape[2]
    hidden = experts_local * ff
    experts = experts_local * peers
    part = tokens.shape[2]
    section = lax.axis_index("section")
    index = lax.axis_index("expert")
    chip, core = lax.div(index, 2), lax.rem(index, 2)
    other = 1 - core
    sibling = chip * 2 + other

    def slot_of(chip_index, core_index):
        return core_index * chips + chip_index

    mine = slot_of(chip, core)

    def weight_copies(which):
        copies = []
        for e in range(experts_local):
            if which < 2:
                source = (gate_hbm, up_hbm)[which]
                copies.append(pltpu.make_async_copy(
                    source.at[e], w_in.at[:, pl.ds((2 * e + which) * ff, ff)],
                    weight_sem.at[which, e]))
            else:
                copies.append(pltpu.make_async_copy(
                    down_hbm.at[e], w_down.at[pl.ds(e * ff, ff)], weight_sem.at[which, e]))
        return copies

    for copy in weight_copies(0) + weight_copies(1) + weight_copies(2):
        copy.start()

    def remote(source, target, send, recv, device):
        return pltpu.make_async_remote_copy(
            src_ref=source, dst_ref=target, send_sem=send, recv_sem=recv,
            device_id=device, device_id_type=MESH)

    def at_peer(peer):
        return {"section": section, "expert": peer}

    def at_section(which):
        return {"section": which, "expert": index}

    barrier = pltpu.get_barrier_semaphore()
    for step in range(1, peers):
        pl.semaphore_signal(barrier, inc=1, device_id=at_peer(lax.rem(index + step, peers)),
                            device_id_type=MESH)
    for step in range(1, sections):
        pl.semaphore_signal(barrier, inc=1,
                            device_id=at_section(lax.rem(section + step, sections)),
                            device_id_type=MESH)
    pl.semaphore_wait(barrier, peers + sections - 2)

    def token_copy(g, origin):
        columns = pl.ds(pl.multiple_of(origin * part, part), part)
        return remote(tokens.at[g], x_in.at[g, :, columns], token_send.at[g],
                      token_recv.at[g, origin], at_section(0))

    @pl.when(section > 0)
    def _():
        for g in range(groups):
            token_copy(g, section).start()

    lane = lax.broadcasted_iota(jnp.int32, (rows, LANES), 1)
    spread = jnp.zeros((rows, LANES), jnp.float32)
    top = ids.shape[2]
    for g in range(groups):
        share = probs[g] / jnp.sum(probs[g], axis=-1, keepdims=True)
        named = ids[g] + g * experts
        for k in range(top):
            spread += jnp.where(named[:, k:k + 1] == lane, share[:, k:k + 1], 0.0)
    shares[mine] = spread

    def share_copy(step):
        target = lax.rem(index + step, peers)
        return remote(shares.at[mine], shares.at[mine], share_send.at[step],
                      share_recv.at[mine], at_peer(target))

    def gather_copy(g, step):
        target = lax.rem(chip + step, chips) * 2 + core
        return remote(normed.at[g, mine], normed.at[g, mine], gather_send.at[g, step],
                      gather_recv.at[g, mine], at_peer(target))

    def sibling_copy(g):
        return remote(normed.at[g, mine], normed.at[g, mine], gather_send.at[g, 0],
                      gather_recv.at[g, mine], at_peer(sibling))

    def forward_copy(g, step):
        slot = slot_of(lax.rem(chip + step, chips), core)
        return remote(normed.at[g, slot], normed.at[g, slot], forward_send.at[g, step],
                      gather_recv.at[g, slot], at_peer(sibling))

    def gather_arrival(g, slot):
        return remote(normed.at[g, slot], normed.at[g, slot], gather_send.at[g, 0],
                      gather_recv.at[g, slot], at_peer(sibling))

    half = width // HALVES

    def pair_copy(g, h):
        return remote(partial.at[g, h, pl.ds(other * chips, chips)], pair_in.at[g, h],
                      pair_send.at[g, h], pair_recv.at[g, h], at_peer(sibling))

    def return_copy(g, h, step):
        target = lax.rem(chip + step, chips)
        return remote(pair_out.at[g, h, target], returned.at[g, h, chip],
                      return_send.at[g, h, step], return_recv.at[g, h, chip],
                      at_peer(target * 2 + core))

    def return_arrival(g, h, origin):
        return remote(pair_out.at[g, h, origin], returned.at[g, h, origin],
                      return_send.at[g, h, 0], return_recv.at[g, h, origin], at_peer(sibling))

    def pass_copy(g, h):
        columns = pl.ds(h * half, half)
        return remote(out.at[g, :, columns], x_in.at[g, :, columns], pass_send.at[g, h],
                      pass_recv.at[g, h], at_section(lax.rem(section + 1, sections)))

    def enter(g):
        @pl.when(section == 0)
        def _():
            x_in[g, :, pl.ds(0, part)] = tokens[g]
            for origin in range(1, sections):
                token_copy(g, origin).wait_recv()

        @pl.when(section > 0)
        def _():
            for h in range(HALVES):
                pass_copy(g, h).wait_recv()

        wide = x_in[g].astype(jnp.float32)
        scale = lax.rsqrt(jnp.mean(wide * wide, axis=-1, keepdims=True) + EPS)
        normed[g, mine] = (wide * scale * gain[...]).astype(jnp.bfloat16)
        for step in range(1, chips):
            gather_copy(g, step).start()
        sibling_copy(g).start()

    def forward(g):
        for step in range(1, chips):
            gather_arrival(g, slot_of(lax.rem(chip + step, chips), core)).wait_recv()
            forward_copy(g, step).start()

    total_rows = peers * rows
    slots = CAP * (total_rows // BLOCK)
    all_slots = experts_local * slots
    wide_lane = lax.broadcasted_iota(jnp.int32, (total_rows, LANES), 1)
    slot_lane = lax.broadcasted_iota(jnp.int32, (total_rows, all_slots), 1).astype(jnp.float32)

    def project_in(g):
        @pl.when(g == 0)
        def _():
            for step in range(1, peers):
                origin = lax.rem(index + step, peers)
                slot = slot_of(lax.div(origin, 2), lax.rem(origin, 2))
                remote(shares.at[slot], shares.at[slot], share_send.at[step],
                       share_recv.at[slot], at_peer(origin)).wait_recv()

        every = shares[...].reshape(total_rows, LANES)
        below = (lax.broadcasted_iota(jnp.int32, (total_rows, total_rows), 0)
                 > lax.broadcasted_iota(jnp.int32, (total_rows, total_rows), 1))
        ranks = jnp.dot(jnp.where(below, 1.0, 0.0).astype(jnp.bfloat16),
                        jnp.where(every > 0.0, 1.0, 0.0).astype(jnp.bfloat16),
                        preferred_element_type=jnp.float32)
        weighted = jnp.zeros((total_rows, all_slots), jnp.float32)
        for e in range(experts_local):
            pick = wide_lane == g * experts + index * experts_local + e
            factor = jnp.sum(jnp.where(pick, every, 0.0), axis=-1, keepdims=True)
            rank = jnp.sum(jnp.where(pick, ranks, 0.0), axis=-1, keepdims=True)
            inside = (slot_lane >= e * slots) & (slot_lane < (e + 1) * slots)
            weighted += jnp.where(inside & (rank + e * slots == slot_lane), factor, 0.0)
        chosen[...] = jnp.where(weighted > 0.0, 1.0, 0.0).astype(jnp.bfloat16)
        flipped = weighted.T
        slot_share = jnp.sum(flipped, axis=-1, keepdims=True)
        picker = jnp.where(flipped > 0.0, 1.0, 0.0).astype(jnp.bfloat16)

        for step in range(chips):
            gather_arrival(g, slot_of(lax.rem(chip + step, chips), other)).wait_recv()

        @pl.when(g == 0)
        def _():
            for copy in weight_copies(0) + weight_copies(1):
                copy.wait()

        rows_in = jnp.dot(picker, normed[g].reshape(total_rows, width),
                          preferred_element_type=jnp.float32).astype(jnp.bfloat16)
        for e in range(experts_local):
            span = slice(e * slots, (e + 1) * slots)
            both = jnp.dot(rows_in[span], w_in[:, pl.ds(2 * e * ff, 2 * ff)],
                           preferred_element_type=jnp.float32)
            gate, up = both[:, :ff], both[:, ff:]
            mid = gate / (1.0 + jnp.exp(-gate)) * up * slot_share[span]
            active[e] = mid.astype(jnp.bfloat16)

    def project_out(g, h):
        if h == 0:
            @pl.when(g == 0)
            def _():
                for copy in weight_copies(2):
                    copy.wait()

        columns = pl.ds(h * half, half)
        pieces = [
            jnp.dot(active[e], w_down[pl.ds(e * ff, ff), columns],
                    preferred_element_type=jnp.float32).astype(jnp.bfloat16)
            for e in range(experts_local)
        ]
        result = jnp.dot(chosen[...], jnp.concatenate(pieces, axis=0),
                         preferred_element_type=jnp.float32)
        partial[g, h] = result.astype(jnp.bfloat16).reshape(peers, rows, half)
        pair_copy(g, h).start()

    def combine(g, h):
        pair_copy(g, h).wait_recv()
        for step in range(1, chips + 1):
            target = lax.rem(chip + step, chips)
            both = (partial[g, h, slot_of(target, core)].astype(jnp.float32)
                    + pair_in[g, h, target].astype(jnp.float32)).astype(jnp.bfloat16)
            pair_out[g, h, target] = both
            if step < chips:
                return_copy(g, h, step).start()

    def leave(g, h):
        columns = pl.ds(h * half, half)
        total = x_in[g, :, columns].astype(jnp.float32) + pair_out[g, h, chip].astype(jnp.float32)
        for step in range(1, chips):
            origin = lax.rem(chip + step, chips)
            return_arrival(g, h, origin).wait_recv()
            total += returned[g, h, origin].astype(jnp.float32)
        out[g, :, columns] = total.astype(jnp.bfloat16)

        @pl.when(section < sections - 1)
        def _():
            pass_copy(g, h).start()

    for step in range(1, peers):
        share_copy(step).start()

    enter(0)
    ahead = jnp.where(section == 0, 2, 1)

    @pl.when(section == 0)
    def _():
        enter(1)

    forward(0)

    def one(g, carry):
        project_in(g)

        @pl.when(g + ahead < groups)
        def _():
            enter(g + ahead)

        for h in range(HALVES):
            project_out(g, h)
        @pl.when(g > 0)
        def _():
            for h in range(HALVES):
                leave(g - 1, h)

        for h in range(HALVES - 1):
            combine(g, h)

        @pl.when(g < groups - 1)
        def _():
            forward(g + 1)

        combine(g, HALVES - 1)

        return carry

    lax.fori_loop(0, groups, one, 0)
    for h in range(HALVES):
        leave(groups - 1, h)

    for step in range(1, peers):
        share_copy(step).wait_send()

    def drain(g, carry):
        @pl.when(section > 0)
        def _():
            token_copy(g, section).wait_send()

        @pl.when(section < sections - 1)
        def _():
            for h in range(HALVES):
                pass_copy(g, h).wait_send()

        sibling_copy(g).wait_send()
        for step in range(1, chips):
            gather_copy(g, step).wait_send()
            forward_copy(g, step).wait_send()
        for h in range(HALVES):
            pair_copy(g, h).wait_send()
            for step in range(1, chips):
                return_copy(g, h, step).wait_send()
        return carry

    lax.fori_loop(0, groups, drain, 0)


def local(sections, peers, tokens, norm_gain, gate_weight, up_weight, down_weight, expert_ids,
          gate_probs):
    micro, rows_each, part = tokens.shape
    width = norm_gain.shape[1]
    groups, rows = micro // GROUP, rows_each * GROUP
    experts_local, ff = gate_weight.shape[1], gate_weight.shape[3]
    hidden = experts_local * ff
    top = expert_ids.shape[3]
    chips = peers // 2
    slots = CAP * (peers * rows // BLOCK)
    vmem = pl.BlockSpec(memory_space=pltpu.VMEM)
    anywhere = pl.BlockSpec(memory_space=pl.ANY)
    dma = pltpu.SemaphoreType.DMA
    bf16 = jnp.bfloat16
    result = pl.pallas_call(
        functools.partial(kernel, sections, peers, experts_local),
        out_shape=jax.ShapeDtypeStruct((groups, rows, width), bf16),
        in_specs=[vmem, vmem, anywhere, anywhere, anywhere, vmem, vmem],
        out_specs=vmem,
        scratch_shapes=[
            pltpu.VMEM((width, 2 * hidden), bf16),
            pltpu.VMEM((hidden, width), bf16),
            pltpu.VMEM((groups, rows, width), bf16),
            pltpu.VMEM((groups, peers, rows, width), bf16),
            pltpu.VMEM((experts_local, slots, ff), bf16),
            pltpu.VMEM((peers * rows, experts_local * slots), bf16),
            pltpu.VMEM((groups, HALVES, peers, rows, width // HALVES), bf16),
            pltpu.VMEM((groups, HALVES, chips, rows, width // HALVES), bf16),
            pltpu.VMEM((groups, HALVES, chips, rows, width // HALVES), bf16),
            pltpu.VMEM((groups, HALVES, chips, rows, width // HALVES), bf16),
            pltpu.VMEM((peers, rows, LANES), jnp.float32),
            dma((3, experts_local)),
            dma((groups,)),
            dma((groups, sections)),
            dma((peers,)),
            dma((peers,)),
            dma((groups, chips)),
            dma((groups, peers)),
            dma((groups, chips)),
            dma((groups, HALVES)),
            dma((groups, HALVES)),
            dma((groups, HALVES, chips)),
            dma((groups, HALVES, chips)),
            dma((groups, HALVES)),
            dma((groups, HALVES)),
        ],
        compiler_params=pltpu.CompilerParams(
            collective_id=0, has_side_effects=True, vmem_limit_bytes=58 * 2**20
        ),
    )(
        tokens.reshape(groups, rows, part),
        norm_gain,
        gate_weight[0],
        up_weight[0],
        down_weight[0],
        expert_ids[0].reshape(groups, rows, top),
        gate_probs[0].reshape(groups, rows, top),
    )
    return result.reshape(1, micro, rows_each, width)


def solution(mesh):
    in_specs = (
        P(None, "expert", "section"),
        P("section", None),
        P("section", "expert", None, None),
        P("section", "expert", None, None),
        P("section", "expert", None, None),
        P("section", None, "expert", None),
        P("section", None, "expert", None),
    )
    out_specs = P("section", None, "expert", None)
    body = functools.partial(local, mesh.shape["section"], mesh.shape["expert"])
    return jax.shard_map(body, mesh=mesh, in_specs=in_specs, out_specs=out_specs, check_vma=False)
```
